512 devices in a mesh: dp: 64 (over z, x), tensor: 8 (over y, core).
Axes of the slice: x: 4, y: 4, z: 16, core: 2. Of those that a mesh axis runs over, the one named last changes fastest.
Arguments:
- pool: bfloat16 [65536, 4096], P('dp', 'tensor'), may hold values from -6 to 6
- picks: int32 [256], P('dp'), may hold values from 0 to 1023
- targets: bfloat16 [256, 4096], P(None, 'dp'), may hold values from -6 to 6
- gate_weight: bfloat16 [4096, 7168], P('dp', 'tensor'), may hold values from -0.09375 to 0.09375
- up_weight: bfloat16 [4096, 7168], P('dp', 'tensor'), may hold values from -0.09375 to 0.09375
- down_weight: bfloat16 [7168, 4096], P('tensor', 'dp'), may hold values from -0.0625 to 0.0625
- probe_gate: float32 [4096, 7168], P('dp', 'tensor'), may hold values from -6 to 6
- probe_up: float32 [4096, 7168], P('dp', 'tensor'), may hold values from -6 to 6
- probe_down: float32 [7168, 4096], P('tensor', 'dp'), may hold values from -6 to 6
Outputs:
- final_gate: float32 [4096, 7168], P('dp', 'tensor')
- final_up: float32 [4096, 7168], P('dp', 'tensor')
- final_down: float32 [7168, 4096], P('tensor', 'dp')
- rayleigh: float32 [], replicated
The draws below stay inside these ranges and needn't reach their ends.
Inputs may be any that keep to these rules, and one draw needn't show every extreme that they name: `picks`: a token's pool row lies in the block of 1024 rows held by the dp index that owns the token.
All inputs are finite; a program needn't handle non-finite values.
Results may differ from the reference program's by a relative error of at most 0.0085.
Values may be sent and summed in bfloat16 or wider, within the bound.
No kernel may reach another device: no remote copies, remote signals or barrier semaphores. Data moves between devices by JAX's collectives and lax.ppermute only.
A program may use at most 64 MiB of HBM per device.

```python
import jax
import jax.numpy as jnp

D = 4096
FF = 7168
TOK_DEV = 4
POOL_DEV = 1024
ITERS = 2
TOKENS = 256
POOL = 65536


def set_ends(array, key, least, top_value):
    longest = array.shape.index(max(array.shape))
    spots = []
    for shift in (0, 1):
        where = [jax.random.randint(jax.random.fold_in(key, axis), (), 0, length) for axis, length in enumerate(array.shape)]
        where[longest] = (where[longest] + shift) % array.shape[longest]
        spots.append(tuple(where))
    return array.at[spots[0]].set(least).at[spots[1]].set(top_value)


def block_levels(stream_key, extent, split, smallest, high):
    factor_of, own = 1.0, jax.random.fold_in(stream_key, 6)
    for dim, shards_of in split:
        heights = jnp.exp(jax.random.uniform(jax.random.fold_in(own, dim), (shards_of,), jnp.float32, smallest / len(split), high / len(split)))
        factor_of = factor_of * jnp.repeat(heights, extent[dim] // shards_of).reshape([-1 if axis == dim else 1 for axis in range(len(extent))])
    return factor_of


def bell_draw(stream_key, dims, scale, limit, shards=(), held_as=jnp.bfloat16):
    result = jax.random.normal(stream_key, dims, jnp.float32) * scale
    if len(shards) > 0:
        result = block_levels(stream_key, dims, shards, -0.22, 0.18) * result
    return jnp.clip(result, min=-limit, max=limit).astype(held_as)


def setup_inputs(seed: int = 0) -> dict:
    arg_keys = jax.random.split(jax.random.key(seed), 10)
    return {
        "pool": bell_draw(arg_keys[0], (POOL, D), 1.0, 6.0, ((0, 64), (1, 8))),
        "picks": set_ends(jax.random.randint(arg_keys[1], (TOKENS,), 0, POOL_DEV), jax.random.fold_in(arg_keys[1], 1), 0, POOL_DEV - 1).astype(jnp.int32),
        "targets": bell_draw(arg_keys[2], (TOKENS, D), 1.0, 6.0, ((1, 64),)),
        "gate_weight": bell_draw(arg_keys[3], (D, FF), D ** -0.5, 0.09375, ((0, 64), (1, 8))),
        "up_weight": bell_draw(arg_keys[4], (D, FF), D ** -0.5, 0.09375, ((0, 64), (1, 8))),
        "down_weight": bell_draw(arg_keys[5], (FF, D), FF ** -0.5, 0.0625, ((0, 8), (1, 64))),
        "probe_gate": bell_draw(arg_keys[6], (D, FF), 1.0, 6.0, ((0, 64), (1, 8)), jnp.float32),
        "probe_up": bell_draw(arg_keys[7], (D, FF), 1.0, 6.0, ((0, 64), (1, 8)), jnp.float32),
        "probe_down": bell_draw(arg_keys[8], (FF, D), 1.0, 6.0, ((0, 8), (1, 64)), jnp.float32),
    }


def silu_parts(values):
    sigmoid_val = jax.nn.sigmoid(values)
    activated = values * sigmoid_val
    slope_one = sigmoid_val * (1.0 + values * (1.0 - sigmoid_val))
    slope_two = sigmoid_val * (1.0 - sigmoid_val) * (2.0 + values * (1.0 - 2.0 * sigmoid_val))
    return (activated, slope_one, slope_two)

def matmul_plain(former, latter):
    return jnp.dot(former, latter, preferred_element_type=jnp.float32)

def reference(pool, picks, targets, gate_weight, up_weight, down_weight, probe_gate, probe_up, probe_down):
    rows = jnp.arange(TOKENS, dtype=jnp.int32) // TOK_DEV * POOL_DEV + picks.astype(jnp.int32)
    inputs = jnp.take(pool, rows, axis=0)
    gate_val = matmul_plain(inputs, gate_weight)
    upper_val = matmul_plain(inputs, up_weight)
    activated, slope_one, slope_two = silu_parts(gate_val)
    hidden = (activated * upper_val).astype(jnp.bfloat16)
    output = matmul_plain(hidden, down_weight)
    resid_b = ((output - targets.astype(jnp.float32)) / TOKENS).astype(jnp.bfloat16)
    back_val = matmul_plain(resid_b, down_weight.T)
    back_act = back_val * upper_val
    count = 3.0 * D * FF
    vectors = (probe_gate, probe_up, probe_down)
    quotient = jnp.zeros((), jnp.float32)
    for iteration in range(ITERS):
        gate_probe = vectors[0].astype(jnp.bfloat16)
        upper_probe = vectors[1].astype(jnp.bfloat16)
        down_probe = vectors[2].astype(jnp.bfloat16)
        tan_gate = matmul_plain(inputs, gate_probe)
        tan_upper = matmul_plain(inputs, upper_probe)
        tan_act = slope_one * tan_gate
        tan_hidden = (tan_act * upper_val + activated * tan_upper).astype(jnp.bfloat16)
        tan_out = matmul_plain(tan_hidden, down_weight) + matmul_plain(hidden, down_probe)
        tan_resid = (tan_out / TOKENS).astype(jnp.bfloat16)
        hv_down = matmul_plain(tan_hidden.T, resid_b) + matmul_plain(hidden.T, tan_resid)
        tan_back = matmul_plain(tan_resid, down_weight.T) + matmul_plain(resid_b, down_probe.T)
        delta_up = (tan_back * activated + back_val * tan_act).astype(jnp.bfloat16)
        delta_gate = ((tan_back * upper_val + back_val * tan_upper) * slope_one + back_act * slope_two * tan_gate).astype(jnp.bfloat16)
        hv_gate = matmul_plain(inputs.T, delta_gate)
        hv_up = matmul_plain(inputs.T, delta_up)
        square = jnp.sum(hv_gate * hv_gate) + jnp.sum(hv_up * hv_up) + jnp.sum(hv_down * hv_down)
        if iteration + 1 == ITERS:
            inner = jnp.sum(vectors[0] * hv_gate) + jnp.sum(vectors[1] * hv_up) + jnp.sum(vectors[2] * hv_down)
            quotient = inner / count
        norm_val = jnp.sqrt(square / count + 1e-06)
        vectors = (hv_gate / norm_val, hv_up / norm_val, hv_down / norm_val)
    return (vectors[0], vectors[1], vectors[2], quotient)
```

```python
import jax
import jax.numpy as jnp
from jax import lax
from jax.sharding import Mesh
from jax.sharding import PartitionSpec as P

AXES = ("z", "x", "y", "core")
SIZES = (16, 4, 4, 2)
XYC = ("x", "y", "core")
BF = jnp.bfloat16
F32 = jnp.float32


def dot(a, b, ca, cb):
    return lax.dot_general(a, b, (((ca,), (cb,)), ((), ())), preferred_element_type=F32)


def exchange(v, axes):
    return lax.all_to_all(v, axes, split_axis=0, concat_axis=0, tiled=True)


def gather(v, axes, n):
    return exchange(jnp.broadcast_to(v[None], (n,) + v.shape), axes)


def two_terms(v):
    high = lax.reduce_precision(v, 8, 7)
    return high.astype(BF), (v - high).astype(BF)


def silu_parts(values):
    s = jax.nn.sigmoid(values)
    activated = values * s
    slope_one = s * (1.0 + values * (1.0 - s))
    slope_two = s * (1.0 - s) * (2.0 + values * (1.0 - 2.0 * s))
    return activated, slope_one, slope_two


def make_body(nz, nx, ny, nc):
    nt = ny * nc
    nr = nx * nt

    def body(pool, picks, targets, gate_w, up_w, down_w, probe_g, probe_u, probe_d):
        tok_dev = picks.shape[0]
        tokens = targets.shape[0]
        d_dev, ff_dev = gate_w.shape
        ff = ff_dev // nx
        dz = d_dev * nx
        sub = ff // nz
        rows = dz // nr
        count = 3.0 * (dz * nz) * (ff_dev * nt)

        chosen = pool.at[picks].get(mode="promise_in_bounds")
        wide = gather(chosen, ("y", "core"), nt)
        wide = wide.transpose(1, 0, 2).reshape(tok_dev, nz, dz).transpose(1, 0, 2)
        wide = jnp.broadcast_to(wide[:, None], (nz, nx, tok_dev, dz))
        inputs = exchange(wide.reshape(nz * nx, tok_dev, dz), ("z", "x")).reshape(tokens, dz)

        mats = jnp.stack(
            [
                gate_w,
                up_w,
                probe_g.astype(BF),
                probe_u.astype(BF),
                down_w.T,
                probe_d.T.astype(BF),
            ]
        )
        mats = mats.reshape(6, d_dev, nx, ff).transpose(2, 0, 1, 3)
        mats = exchange(mats, "x").transpose(1, 0, 2, 3).reshape(6, dz, ff)
        down, pdown = mats[4], mats[5]

        first = lax.dot_general(
            mats[:4], inputs, (((1,), (1,)), ((), ())), preferred_element_type=F32
        )
        own = lax.axis_index(XYC)
        gram_rows = tokens // nr
        mine = lax.dynamic_slice_in_dim(inputs, own * gram_rows, gram_rows, 0)
        gram = jnp.concatenate(two_terms(dot(mine, inputs, 1, 1)))
        packed = first.astype(BF).reshape(4, nz, sub, tokens).transpose(1, 0, 2, 3)
        packed = packed.reshape(nz, 4 * sub, tokens)
        packed = jnp.concatenate(
            [packed, jnp.broadcast_to(gram[None], (nz,) + gram.shape)], axis=1
        )
        got = jnp.sum(exchange(packed, "z").astype(F32), axis=0)
        gate_val, upper, tan_gate, tan_upper = (
            got[i * sub : (i + 1) * sub] for i in range(4)
        )
        gram = got[4 * sub : 4 * sub + gram_rows] + got[4 * sub + gram_rows :]
        activated, slope_one, slope_two = silu_parts(gate_val)
        hidden = (activated * upper).astype(BF)
        tan_act = slope_one * tan_gate
        tan_hidden = (tan_act * upper + activated * tan_upper).astype(BF)
        both = gather(jnp.concatenate([hidden, tan_hidden]), "z", nz)
        hidden = both[:, :sub].reshape(ff, tokens)
        tan_hidden = both[:, sub:].reshape(ff, tokens)

        out = dot(down, hidden, 1, 0)
        tan_out = dot(down, tan_hidden, 1, 0) + dot(pdown, hidden, 1, 0)
        packed = jnp.stack([out.astype(BF), tan_out.astype(BF)])
        packed = packed.reshape(2, nr, rows, tokens).transpose(1, 0, 2, 3)
        got = jnp.sum(exchange(packed, XYC).astype(F32), axis=0)
        wanted = lax.dynamic_slice_in_dim(
            targets.T, lax.axis_index(("y", "core")) * rows, rows, 0
        )
        resid = ((got[0] - wanted.astype(F32)) / tokens).astype(BF)
        tan_resid = (got[1] / tokens).astype(BF)
        packed = jnp.concatenate([resid, tan_resid, *two_terms(gram)])
        both = gather(packed, XYC, nr)
        resid = both[:, :rows].reshape(dz, tokens)
        tan_resid = both[:, rows : 2 * rows].reshape(dz, tokens)
        gram_hi = both[:, 2 * rows : 2 * rows + gram_rows].reshape(tokens, tokens)
        gram_lo = both[:, 2 * rows + gram_rows :].reshape(tokens, tokens)

        def by_gram(v):
            return dot(v, gram_hi, 1, 0) + dot(v, gram_lo, 1, 0)

        back = dot(down, resid, 0, 0)
        tan_back = dot(down, tan_resid, 0, 0) + dot(pdown, resid, 0, 0)
        packed = jnp.stack([back.astype(BF), tan_back.astype(BF)])
        packed = packed.reshape(2, nz, sub, tokens).transpose(1, 0, 2, 3)
        got = jnp.sum(exchange(packed, "z").astype(F32), axis=0)
        back, tan_back = got[0], got[1]
        hv_down = dot(resid, tan_hidden, 1, 1) + dot(tan_resid, hidden, 1, 1)

        def deltas(tan_back, tan_gate, tan_upper):
            up = tan_back * activated + back * (slope_one * tan_gate)
            gate = (tan_back * upper + back * tan_upper) * slope_one + (
                back * upper
            ) * slope_two * tan_gate
            return jnp.concatenate([gate.astype(BF), up.astype(BF)])

        delta = deltas(tan_back, tan_gate, tan_upper)

        tangents = by_gram(delta)
        square = jnp.sum(delta.astype(F32) * tangents) + jnp.sum(hv_down * hv_down)
        tan_gate, tan_upper = tangents[:sub], tangents[sub:]
        tan_hidden = ((slope_one * tan_gate) * upper + activated * tan_upper).astype(BF)

        def rows_of(*values):
            terms = [t for v in values for t in two_terms(v)]
            return jnp.stack([jnp.broadcast_to(t, (tokens,)) for t in terms])

        both = gather(jnp.concatenate([tan_hidden, rows_of(square)]), "z", nz)
        tan_hidden = both[:, :sub].reshape(ff, tokens)
        square = jnp.sum(both[:, sub:, 0].astype(F32))

        hv_down_b = hv_down.astype(BF)
        tan_out = dot(down, tan_hidden, 1, 0) + dot(hv_down_b, hidden, 1, 0)
        packed = tan_out.astype(BF).reshape(nr, rows, tokens)
        scal = jnp.broadcast_to(rows_of(square)[None], (nr, 2, tokens))
        got = exchange(jnp.concatenate([packed, scal], axis=1), XYC)
        square = jnp.sum(got[:, rows:, 0].astype(F32))
        got = jnp.sum(got[:, :rows].astype(F32), axis=0)
        scale = 1.0 / jnp.sqrt(square / count + 1e-6)
        tan_resid = (got / tokens).astype(BF)
        tan_resid = gather(tan_resid, XYC, nr).reshape(dz, tokens)

        tan_back = dot(down, tan_resid, 0, 0) + dot(hv_down_b, resid, 0, 0)
        packed = tan_back.astype(BF).reshape(nz, sub, tokens)
        tan_back = jnp.sum(exchange(packed, "z").astype(F32), axis=0)
        hv_down2 = (dot(resid, tan_hidden, 1, 1) + dot(tan_resid, hidden, 1, 1)) * scale

        tangents = tangents * scale
        delta = deltas(tan_back * scale, tangents[:sub], tangents[sub:])
        wide = delta.astype(F32)
        inner = jnp.sum(tangents * wide) + jnp.sum((hv_down * scale) * hv_down2)
        square = jnp.sum(by_gram(delta) * wide) + jnp.sum(hv_down2 * hv_down2)
        both = gather(jnp.concatenate([delta, rows_of(inner, square)]), "z", nz)
        delta_gate = both[:, :sub].reshape(ff, tokens)
        delta_up = both[:, sub : 2 * sub].reshape(ff, tokens)
        inner = jnp.sum(both[:, 2 * sub : 2 * sub + 2, 0].astype(F32))
        square = jnp.sum(both[:, 2 * sub + 2 :, 0].astype(F32))
        sums = jnp.stack([inner, square])
        sums = jnp.broadcast_to(sums[:, None], (2, 128))
        sums = jnp.sum(gather(sums, XYC, nr), axis=0)
        inner, square = sums[0, 0], sums[1, 0]
        scale = 1.0 / jnp.sqrt(square / count + 1e-6)

        hv = jnp.stack(
            [
                dot(inputs, delta_gate, 0, 1).astype(BF),
                dot(inputs, delta_up, 0, 1).astype(BF),
                hv_down2.astype(BF),
            ]
        )
        hv = hv.reshape(3, nx, d_dev, ff).transpose(1, 0, 2, 3)
        hv = exchange(hv, "x").transpose(1, 2, 0, 3).reshape(3, d_dev, ff_dev)
        hv = hv.astype(F32) * scale
        return hv[0], hv[1], hv[2].T, inner / count

    return body


def build(devices, sizes):
    wide = Mesh(devices.reshape(sizes), AXES)
    dp, tensor = ("z", "x"), ("y", "core")
    placed = (
        P(dp, tensor),
        P(dp),
        P(None, dp),
        P(dp, tensor),
        P(dp, tensor),
        P(tensor, dp),
        P(dp, tensor),
        P(dp, tensor),
        P(tensor, dp),
    )
    return jax.shard_map(
        make_body(*sizes),
        mesh=wide,
        in_specs=placed,
        out_specs=(P(dp, tensor), P(dp, tensor), P(tensor, dp), P()),
        check_vma=False,
    )


def solution(mesh):
    return build(mesh.devices, SIZES)
```

```python
import jax
import jax.numpy as jnp
from jax import lax
from jax.sharding import Mesh
from jax.sharding import PartitionSpec as P

AXES = ("zh", "zl", "x", "y", "core")
SIZES = (8, 2, 4, 4, 2)
NEAR = ("zl", "x")
REST = ("zl", "x", "y", "core")
BF = jnp.bfloat16
F32 = jnp.float32


def dot(a, b, ca, cb):
    return lax.dot_general(a, b, (((ca,), (cb,)), ((), ())), preferred_element_type=F32)


def exchange(v, axes):
    return lax.all_to_all(v, axes, split_axis=0, concat_axis=0, tiled=True)


def gather(v, axes, n):
    return exchange(jnp.broadcast_to(v[None], (n,) + v.shape), axes)


def two_terms(v):
    high = lax.reduce_precision(v, 8, 7)
    return high.astype(BF), (v - high).astype(BF)


def silu_parts(values):
    s = jax.nn.sigmoid(values)
    activated = values * s
    slope_one = s * (1.0 + values * (1.0 - s))
    slope_two = s * (1.0 - s) * (2.0 + values * (1.0 - 2.0 * s))
    return activated, slope_one, slope_two


def total(v):
    ones = jnp.ones((v.shape[1], 128), F32)
    both = lax.dot_general(
        v, ones, (((1,), (0,)), ((), ())), precision=lax.Precision.HIGHEST, preferred_element_type=F32
    )
    return both[:, :1]


def make_body(nz, nl, nx, ny, nc):
    nt = ny * nc
    nx = nl * nx
    nr = nx * nt

    def body(pool, picks, targets, gate_w, up_w, down_w, probe_g, probe_u, probe_d):
        tok_dev = picks.shape[0]
        tokens = targets.shape[0]
        d_dev, ff_dev = gate_w.shape
        ff = ff_dev // nx
        dz = d_dev * nx
        sub = ff // nz
        rows = dz // nr
        count = 3.0 * (dz * nz) * (ff_dev * nt)

        chosen = pool.at[picks].get(mode="promise_in_bounds")
        wide = gather(chosen, ("y", "core"), nt)
        wide = wide.transpose(1, 0, 2).reshape(tok_dev, nz, dz).transpose(1, 0, 2)
        wide = jnp.broadcast_to(wide[:, None], (nz, nx, tok_dev, dz))
        inputs = exchange(wide.reshape(nz * nx, tok_dev, dz), ("zh", *NEAR)).reshape(tokens, dz)

        mats = jnp.stack(
            [
                gate_w,
                up_w,
                probe_g.astype(BF),
                probe_u.astype(BF),
                down_w.T,
                probe_d.T.astype(BF),
            ]
        )
        mats = mats.reshape(6, d_dev, nx, ff).transpose(2, 0, 1, 3)
        mats = exchange(mats, NEAR).transpose(1, 0, 2, 3).reshape(6, dz, ff)
        down, pdown = mats[4], mats[5]

        first = lax.dot_general(
            mats[:4], inputs, (((1,), (1,)), ((), ())), preferred_element_type=F32
        )
        own = lax.axis_index(REST)
        gram_rows = tokens // nr
        mine = lax.dynamic_slice_in_dim(inputs, own * gram_rows, gram_rows, 0)
        gram = jnp.concatenate(two_terms(dot(mine, inputs, 1, 1)))
        packed = first.astype(BF).reshape(4, nz, sub, tokens).transpose(1, 0, 2, 3)
        packed = packed.reshape(nz, 4 * sub, tokens)
        packed = jnp.concatenate(
            [packed, jnp.broadcast_to(gram[None], (nz,) + gram.shape)], axis=1
        )
        got = jnp.sum(exchange(packed, "zh").astype(F32), axis=0)
        gate_val, upper, tan_gate, tan_upper = (
            got[i * sub : (i + 1) * sub] for i in range(4)
        )
        gram = got[4 * sub : 4 * sub + gram_rows] + got[4 * sub + gram_rows :]
        activated, slope_one, slope_two = silu_parts(gate_val)
        hidden = (activated * upper).astype(BF)
        tan_act = slope_one * tan_gate
        tan_hidden = (tan_act * upper + activated * tan_upper).astype(BF)
        both = gather(jnp.concatenate([hidden, tan_hidden]), "zh", nz)
        hidden = both[:, :sub].reshape(ff, tokens)
        tan_hidden = both[:, sub:].reshape(ff, tokens)

        out = dot(down, hidden, 1, 0)
        tan_out = dot(down, tan_hidden, 1, 0) + dot(pdown, hidden, 1, 0)
        packed = jnp.stack([out.astype(BF), tan_out.astype(BF)])
        packed = packed.reshape(2, nr, rows, tokens).transpose(1, 0, 2, 3)
        got = jnp.sum(exchange(packed, REST).astype(F32), axis=0)
        wanted = lax.dynamic_slice_in_dim(
            targets.T, lax.axis_index(("y", "core")) * rows, rows, 0
        )
        resid = ((got[0] - wanted.astype(F32)) / tokens).astype(BF)
        tan_resid = (got[1] / tokens).astype(BF)
        packed = jnp.concatenate([resid, tan_resid, *two_terms(gram)])
        both = gather(packed, REST, nr)
        resid = both[:, :rows].reshape(dz, tokens)
        tan_resid = both[:, rows : 2 * rows].reshape(dz, tokens)
        gram_hi = both[:, 2 * rows : 2 * rows + gram_rows].reshape(tokens, tokens)
        gram_lo = both[:, 2 * rows + gram_rows :].reshape(tokens, tokens)

        def by_gram(v):
            return dot(v, gram_hi, 1, 0) + dot(v, gram_lo, 1, 0)

        back = dot(down, resid, 0, 0)
        tan_back = dot(down, tan_resid, 0, 0) + dot(pdown, resid, 0, 0)
        packed = jnp.stack([back.astype(BF), tan_back.astype(BF)])
        packed = packed.reshape(2, nz, sub, tokens).transpose(1, 0, 2, 3)
        got = jnp.sum(exchange(packed, "zh").astype(F32), axis=0)
        back, tan_back = got[0], got[1]
        hv_down = dot(resid, tan_hidden, 1, 1) + dot(tan_resid, hidden, 1, 1)

        def deltas(tan_back, tan_gate, tan_upper):
            up = tan_back * activated + back * (slope_one * tan_gate)
            gate = (tan_back * upper + back * tan_upper) * slope_one + (
                back * upper
            ) * slope_two * tan_gate
            return jnp.concatenate([gate.astype(BF), up.astype(BF)])

        delta = deltas(tan_back, tan_gate, tan_upper)

        def lanes(v):
            v = jnp.sum(v, axis=0, keepdims=True)
            return jnp.pad(v, ((0, 0), (0, tokens - v.shape[1])))

        def terms(*values):
            return jnp.concatenate([t for v in values for t in two_terms(v)])

        tangents = by_gram(delta)
        square = lanes(delta.astype(F32) * tangents) + lanes(hv_down * hv_down)
        tan_gate, tan_upper = tangents[:sub], tangents[sub:]
        tan_hidden = ((slope_one * tan_gate) * upper + activated * tan_upper).astype(BF)
        both = gather(jnp.concatenate([tan_hidden, terms(square)]), "zh", nz)
        tan_hidden = both[:, :sub].reshape(ff, tokens)
        square = jnp.sum(both[:, sub:].astype(F32), axis=(0, 1))[None]

        hv_down_b = hv_down.astype(BF)
        tan_out = dot(down, tan_hidden, 1, 0) + dot(hv_down_b, hidden, 1, 0)
        packed = tan_out.astype(BF).reshape(nr, rows, tokens)
        scal = jnp.broadcast_to(terms(square)[None], (nr, 2, tokens))
        got = exchange(jnp.concatenate([packed, scal], axis=1), REST)
        square = jnp.sum(got[:, rows:].astype(F32), axis=(0, 1))[None]
        got = jnp.sum(got[:, :rows].astype(F32), axis=0)
        scale = 1.0 / jnp.sqrt(total(square) / count + 1e-6)
        tan_resid = (got / tokens).astype(BF)
        tan_resid = gather(tan_resid, REST, nr).reshape(dz, tokens)

        tan_back = dot(down, tan_resid, 0, 0) + dot(hv_down_b, resid, 0, 0)
        packed = tan_back.astype(BF).reshape(nz, sub, tokens)
        tan_back = jnp.sum(exchange(packed, "zh").astype(F32), axis=0)
        hv_down2 = (dot(resid, tan_hidden, 1, 1) + dot(tan_resid, hidden, 1, 1)) * scale

        tangents = tangents * scale
        delta = deltas(tan_back * scale, tangents[:sub], tangents[sub:])
        wide = delta.astype(F32)
        inner = lanes(tangents * wide) + lanes((hv_down * scale) * hv_down2)
        square = lanes(by_gram(delta) * wide) + lanes(hv_down2 * hv_down2)
        both = gather(jnp.concatenate([delta, terms(inner, square)]), "zh", nz)
        delta_gate = both[:, :sub].reshape(ff, tokens)
        delta_up = both[:, sub : 2 * sub].reshape(ff, tokens)
        sums = both[:, 2 * sub :].reshape(nz, 2, 2, tokens).astype(F32)
        sums = jnp.sum(gather(jnp.sum(sums, axis=(0, 2)), REST, nr), axis=0)
        scale = 1.0 / jnp.sqrt(total(sums[1:]) / count + 1e-6)

        hv = jnp.stack(
            [
                dot(inputs, delta_gate, 0, 1).astype(BF),
                dot(inputs, delta_up, 0, 1).astype(BF),
                hv_down2.astype(BF),
            ]
        )
        hv = hv.reshape(3, nx, d_dev, ff).transpose(1, 0, 2, 3)
        hv = exchange(hv, NEAR).transpose(1, 2, 0, 3).reshape(3, d_dev, ff_dev)
        hv = hv.astype(F32) * scale
        return hv[0], hv[1], hv[2].T, jnp.sum(sums[0]) / count

    return body


def build(devices, sizes):
    wide = Mesh(devices.reshape(sizes), AXES)
    dp, tensor = ("zh", *NEAR), ("y", "core")
    placed = (
        P(dp, tensor),
        P(dp),
        P(None, dp),
        P(dp, tensor),
        P(dp, tensor),
        P(tensor, dp),
        P(dp, tensor),
        P(dp, tensor),
        P(tensor, dp),
    )
    return jax.shard_map(
        make_body(*sizes),
        mesh=wide,
        in_specs=placed,
        out_specs=(P(dp, tensor), P(dp, tensor), P(tensor, dp), P()),
        check_vma=False,
    )


def solution(mesh):
    return build(mesh.devices, SIZES)
```

```python
import jax
import jax.numpy as jnp
from jax import lax
from jax.sharding import Mesh
from jax.sharding import PartitionSpec as P

AXES = ("zh", "zl", "x", "y", "core")
SIZES = (8, 2, 4, 4, 2)
NEAR = ("zl", "x")
REST = ("zl", "x", "y", "core")
LANES = 128
BF = jnp.bfloat16
F32 = jnp.float32


def dot(a, b, ca, cb):
    return lax.dot_general(a, b, (((ca,), (cb,)), ((), ())), preferred_element_type=F32)


def exchange(v, axes):
    return lax.all_to_all(v, axes, split_axis=0, concat_axis=0, tiled=True)


def gather(v, axes, n):
    return exchange(jnp.broadcast_to(v[None], (n,) + v.shape), axes)


def two_terms(v):
    high = lax.reduce_precision(v, 8, 7)
    return high.astype(BF), (v - high).astype(BF)


def silu_parts(values):
    s = jax.nn.sigmoid(values)
    activated = values * s
    slope_one = s * (1.0 + values * (1.0 - s))
    slope_two = s * (1.0 - s) * (2.0 + values * (1.0 - 2.0 * s))
    return activated, slope_one, slope_two


def total(v):
    ones = jnp.ones((v.shape[1], 128), F32)
    both = lax.dot_general(
        v, ones, (((1,), (0,)), ((), ())), precision=lax.Precision.HIGHEST, preferred_element_type=F32
    )
    return both[:, :1]


def make_body(nz, nl, nx, ny, nc):
    nt = ny * nc
    nx = nl * nx
    nr = nx * nt

    def body(pool, picks, targets, gate_w, up_w, down_w, probe_g, probe_u, probe_d):
        tok_dev = picks.shape[0]
        tokens = targets.shape[0]
        d_dev, ff_dev = gate_w.shape
        ff = ff_dev // nx
        dz = d_dev * nx
        sub = ff // nz
        rows = dz // nr
        count = 3.0 * (dz * nz) * (ff_dev * nt)

        chosen = pool.at[picks].get(mode="promise_in_bounds")
        swap = [(i * nt + j, j * nz + i) for i in range(nz) for j in range(nt)]
        chosen = lax.ppermute(chosen, ("zh", "y", "core"), swap)
        inputs = gather(chosen, REST, nr).reshape(tokens, dz)
        targets = targets.reshape(nz, nx, tok_dev, d_dev).transpose(1, 0, 2, 3)
        targets = targets.reshape(tokens, d_dev)

        mats = jnp.stack(
            [
                gate_w,
                up_w,
                probe_g.astype(BF),
                probe_u.astype(BF),
                down_w.T,
                probe_d.T.astype(BF),
            ]
        )
        mats = mats.reshape(6, d_dev, nx, ff).transpose(2, 0, 1, 3)
        mats = exchange(mats, NEAR).transpose(1, 0, 2, 3).reshape(6, dz, ff)
        down, pdown = mats[4], mats[5]

        first = lax.dot_general(
            mats[:4], inputs, (((1,), (1,)), ((), ())), preferred_element_type=F32
        )
        own = lax.axis_index(REST)
        gram_rows = tokens // nr
        mine = lax.dynamic_slice_in_dim(inputs, own * gram_rows, gram_rows, 0)
        gram = jnp.concatenate(two_terms(dot(mine, inputs, 1, 1)))
        packed = first.astype(BF).reshape(4, nz, sub, tokens).transpose(1, 0, 2, 3)
        packed = packed.reshape(nz, 4 * sub, tokens)
        packed = jnp.concatenate(
            [packed, jnp.broadcast_to(gram[None], (nz,) + gram.shape)], axis=1
        )
        got = jnp.sum(exchange(packed, "zh").astype(F32), axis=0)
        gate_val, upper, tan_gate, tan_upper = (
            got[i * sub : (i + 1) * sub] for i in range(4)
        )
        gram = got[4 * sub : 4 * sub + gram_rows] + got[4 * sub + gram_rows :]
        activated, slope_one, slope_two = silu_parts(gate_val)
        hidden = (activated * upper).astype(BF)
        tan_act = slope_one * tan_gate
        tan_hidden = (tan_act * upper + activated * tan_upper).astype(BF)
        both = gather(jnp.concatenate([hidden, tan_hidden]), "zh", nz)
        hidden = both[:, :sub].reshape(ff, tokens)
        tan_hidden = both[:, sub:].reshape(ff, tokens)

        out = dot(down, hidden, 1, 0)
        tan_out = dot(down, tan_hidden, 1, 0) + dot(pdown, hidden, 1, 0)
        packed = jnp.stack([out.astype(BF), tan_out.astype(BF)])
        packed = packed.reshape(2, nr, rows, tokens).transpose(1, 0, 2, 3)
        got = jnp.sum(exchange(packed, REST).astype(F32), axis=0)
        wanted = lax.dynamic_slice_in_dim(
            targets.T, lax.axis_index(("y", "core")) * rows, rows, 0
        )
        resid = ((got[0] - wanted.astype(F32)) / tokens).astype(BF)
        tan_resid = (got[1] / tokens).astype(BF)
        packed = jnp.concatenate([resid, tan_resid, *two_terms(gram)])
        both = gather(packed, REST, nr)
        resid = both[:, :rows].reshape(dz, tokens)
        tan_resid = both[:, rows : 2 * rows].reshape(dz, tokens)
        gram_hi = both[:, 2 * rows : 2 * rows + gram_rows].reshape(tokens, tokens)
        gram_lo = both[:, 2 * rows + gram_rows :].reshape(tokens, tokens)

        def by_gram(v):
            return dot(v, gram_hi, 1, 0) + dot(v, gram_lo, 1, 0)

        back = dot(down, resid, 0, 0)
        tan_back = dot(down, tan_resid, 0, 0) + dot(pdown, resid, 0, 0)
        packed = jnp.stack([back.astype(BF), tan_back.astype(BF)])
        packed = packed.reshape(2, nz, sub, tokens).transpose(1, 0, 2, 3)
        got = jnp.sum(exchange(packed, "zh").astype(F32), axis=0)
        back, tan_back = got[0], got[1]
        hv_down = dot(resid, tan_hidden, 1, 1) + dot(tan_resid, hidden, 1, 1)

        def deltas(tan_back, tan_gate, tan_upper):
            up = tan_back * activated + back * (slope_one * tan_gate)
            gate = (tan_back * upper + back * tan_upper) * slope_one + (
                back * upper
            ) * slope_two * tan_gate
            return jnp.concatenate([gate.astype(BF), up.astype(BF)])

        delta = deltas(tan_back, tan_gate, tan_upper)

        def lanes(v):
            v = jnp.sum(v, axis=0, keepdims=True)
            return jnp.pad(v, ((0, 0), (0, tokens - v.shape[1])))

        def terms(*values):
            return jnp.concatenate([t for v in values for t in two_terms(v)])

        tangents = by_gram(delta)
        square = lanes(delta.astype(F32) * tangents) + lanes(hv_down * hv_down)
        tan_gate, tan_upper = tangents[:sub], tangents[sub:]
        tan_hidden = ((slope_one * tan_gate) * upper + activated * tan_upper).astype(BF)
        both = gather(jnp.concatenate([tan_hidden, terms(square)]), "zh", nz)
        tan_hidden = both[:, :sub].reshape(ff, tokens)
        square = jnp.sum(both[:, sub:].astype(F32), axis=(0, 1))[None]

        hv_down_b = hv_down.astype(BF)
        tan_out = dot(down, tan_hidden, 1, 0) + dot(hv_down_b, hidden, 1, 0)
        packed = tan_out.astype(BF).reshape(nr, rows, tokens)
        scal = jnp.broadcast_to(terms(square)[None], (nr, 2, tokens))
        got = exchange(jnp.concatenate([packed, scal], axis=1), REST)
        square = jnp.sum(got[:, rows:].astype(F32), axis=(0, 1))[None]
        got = jnp.sum(got[:, :rows].astype(F32), axis=0)
        scale = 1.0 / jnp.sqrt(total(square) / count + 1e-6)
        tan_resid = (got / tokens).astype(BF)
        tan_resid = gather(tan_resid, REST, nr).reshape(dz, tokens)

        tan_back = dot(down, tan_resid, 0, 0) + dot(hv_down_b, resid, 0, 0)
        packed = tan_back.astype(BF).reshape(nz, sub, tokens)
        tan_back = jnp.sum(exchange(packed, "zh").astype(F32), axis=0)
        hv_down2 = (dot(resid, tan_hidden, 1, 1) + dot(tan_resid, hidden, 1, 1)) * scale

        tangents = tangents * scale
        delta = deltas(tan_back * scale, tangents[:sub], tangents[sub:])
        wide = delta.astype(F32)
        inner = lanes(tangents * wide) + lanes((hv_down * scale) * hv_down2)
        square = lanes(by_gram(delta) * wide) + lanes(hv_down2 * hv_down2)
        both = gather(jnp.concatenate([delta, terms(inner, square)]), "zh", nz)
        delta_gate = both[:, :sub].reshape(ff, tokens)
        delta_up = both[:, sub : 2 * sub].reshape(ff, tokens)
        sums = both[:, 2 * sub :].reshape(nz, 2, 2, tokens).astype(F32)
        sums = jnp.sum(sums, axis=(0, 2))
        if tokens > LANES:
            sums = sums[:, :LANES] + sums[:, LANES:]
        sums = jnp.pad(sums, ((0, 0), (0, LANES - sums.shape[1])))
        sums = terms(sums)

        hv = [
            jnp.pad(v.reshape(nx, d_dev, ff), ((0, 0), (0, 0), (0, LANES - ff)))
            for v in (
                dot(inputs, delta_gate, 0, 1).astype(BF),
                dot(inputs, delta_up, 0, 1).astype(BF),
                hv_down2.astype(BF),
            )
        ]
        hv.append(jnp.broadcast_to(sums[None], (nx,) + sums.shape))
        got = exchange(jnp.concatenate(hv, axis=1), NEAR)
        sums = jnp.sum(got[:, 3 * d_dev :].astype(F32), axis=0)
        sums = jnp.sum(gather(sums[:2] + sums[2:], ("y", "core"), nt), axis=0)
        scale = 1.0 / jnp.sqrt(total(sums[1:]) / count + 1e-6)
        hv = got[:, : 3 * d_dev, :ff].reshape(nx, 3, d_dev, ff)
        hv = hv.transpose(1, 2, 0, 3).reshape(3, d_dev, ff_dev).astype(F32) * scale
        return hv[0], hv[1], hv[2].T, jnp.sum(sums[0]) / count

    return body


def build(devices, sizes):
    wide = Mesh(devices.reshape(sizes), AXES)
    dp, tensor = ("zh", *NEAR), ("y", "core")
    placed = (
        P(dp, tensor),
        P(dp),
        P(None, dp),
        P(dp, tensor),
        P(dp, tensor),
        P(tensor, dp),
        P(dp, tensor),
        P(dp, tensor),
        P(tensor, dp),
    )
    return jax.shard_map(
        make_body(*sizes),
        mesh=wide,
        in_specs=placed,
        out_specs=(P(dp, tensor), P(dp, tensor), P(tensor, dp), P()),
        check_vma=False,
    )


def solution(mesh):
    return build(mesh.devices, SIZES)
```

```python
import jax
import jax.numpy as jnp
from jax import lax
from jax.sharding import Mesh
from jax.sharding import PartitionSpec as P

AXES = ("zh", "zl", "x", "y", "core")
SIZES = (8, 2, 4, 4, 2)
NEAR = ("zl", "x")
REST = ("zl", "x", "y", "core")
LANES = 128
BF = jnp.bfloat16
F32 = jnp.float32


def dot(a, b, ca, cb):
    return lax.dot_general(a, b, (((ca,), (cb,)), ((), ())), preferred_element_type=F32)


def exchange(v, axes):
    return lax.all_to_all(v, axes, split_axis=0, concat_axis=0, tiled=True)


def gather(v, axes, n):
    return exchange(jnp.broadcast_to(v[None], (n,) + v.shape), axes)


def two_terms(v):
    high = lax.reduce_precision(v, 8, 7)
    return high.astype(BF), (v - high).astype(BF)


def silu_parts(values):
    s = jax.nn.sigmoid(values)
    activated = values * s
    slope_one = s * (1.0 + values * (1.0 - s))
    slope_two = s * (1.0 - s) * (2.0 + values * (1.0 - 2.0 * s))
    return activated, slope_one, slope_two


def total(v):
    ones = jnp.ones((v.shape[1], 128), F32)
    both = lax.dot_general(
        v, ones, (((1,), (0,)), ((), ())), precision=lax.Precision.HIGHEST, preferred_element_type=F32
    )
    return both[:, :1]


def make_body(nz, nl, nx, ny, nc):
    nt = ny * nc
    nx = nl * nx
    nr = nx * nt

    def body(pool, picks, targets, gate_w, up_w, down_w, probe_g, probe_u, probe_d):
        tok_dev = picks.shape[0]
        tokens = targets.shape[0]
        d_dev, ff_dev = gate_w.shape
        ff = ff_dev // nx
        dz = d_dev * nx
        sub = ff // nz
        rows = dz // nr
        count = 3.0 * (dz * nz) * (ff_dev * nt)

        chosen = pool.at[picks].get(mode="promise_in_bounds")
        swap = [(i * nt + j, j * nz + i) for i in range(nz) for j in range(nt)]
        chosen = lax.ppermute(chosen, ("zh", "y", "core"), swap)
        targets = targets.reshape(nz, nx, tok_dev, d_dev).transpose(1, 0, 2, 3)
        targets = targets.reshape(tokens, d_dev)

        mats = jnp.stack(
            [
                gate_w,
                up_w,
                probe_g.astype(BF),
                probe_u.astype(BF),
                down_w.T,
                probe_d.T.astype(BF),
            ]
        )
        mats = mats.reshape(6, d_dev, nx, ff).transpose(2, 0, 1, 3)
        mats = exchange(mats, NEAR)
        chosen, mats = lax.optimization_barrier((chosen, mats))
        mats = mats.transpose(1, 0, 2, 3).reshape(6, dz, ff)
        inputs = gather(chosen, REST, nr).reshape(tokens, dz)
        down, pdown = mats[4], mats[5]

        first = lax.dot_general(
            mats[:4], inputs, (((1,), (1,)), ((), ())), preferred_element_type=F32
        )
        own = lax.axis_index(REST)
        gram_rows = tokens // nr
        mine = lax.dynamic_slice_in_dim(inputs, own * gram_rows, gram_rows, 0)
        gram = jnp.concatenate(two_terms(dot(mine, inputs, 1, 1)))
        packed = first.astype(BF).reshape(4, nz, sub, tokens).transpose(1, 0, 2, 3)
        packed = packed.reshape(nz, 4 * sub, tokens)
        packed = jnp.concatenate(
            [packed, jnp.broadcast_to(gram[None], (nz,) + gram.shape)], axis=1
        )
        got = jnp.sum(exchange(packed, "zh").astype(F32), axis=0)
        gate_val, upper, tan_gate, tan_upper = (
            got[i * sub : (i + 1) * sub] for i in range(4)
        )
        gram = got[4 * sub : 4 * sub + gram_rows] + got[4 * sub + gram_rows :]
        activated, slope_one, slope_two = silu_parts(gate_val)
        hidden = (activated * upper).astype(BF)
        tan_act = slope_one * tan_gate
        tan_hidden = (tan_act * upper + activated * tan_upper).astype(BF)
        both = gather(jnp.concatenate([hidden, tan_hidden]), "zh", nz)
        hidden = both[:, :sub].reshape(ff, tokens)
        tan_hidden = both[:, sub:].reshape(ff, tokens)

        out = dot(down, hidden, 1, 0)
        tan_out = dot(down, tan_hidden, 1, 0) + dot(pdown, hidden, 1, 0)
        packed = jnp.stack([out.astype(BF), tan_out.astype(BF)])
        packed = packed.reshape(2, nr, rows, tokens).transpose(1, 0, 2, 3)
        got = jnp.sum(exchange(packed, REST).astype(F32), axis=0)
        wanted = lax.dynamic_slice_in_dim(
            targets.T, lax.axis_index(("y", "core")) * rows, rows, 0
        )
        resid = ((got[0] - wanted.astype(F32)) / tokens).astype(BF)
        tan_resid = (got[1] / tokens).astype(BF)
        packed = jnp.concatenate([resid, tan_resid, *two_terms(gram)])
        both = gather(packed, REST, nr)
        resid = both[:, :rows].reshape(dz, tokens)
        tan_resid = both[:, rows : 2 * rows].reshape(dz, tokens)
        gram_hi = both[:, 2 * rows : 2 * rows + gram_rows].reshape(tokens, tokens)
        gram_lo = both[:, 2 * rows + gram_rows :].reshape(tokens, tokens)

        def by_gram(v):
            return dot(v, gram_hi, 1, 0) + dot(v, gram_lo, 1, 0)

        back = dot(down, resid, 0, 0)
        tan_back = dot(down, tan_resid, 0, 0) + dot(pdown, resid, 0, 0)
        packed = jnp.stack([back.astype(BF), tan_back.astype(BF)])
        packed = packed.reshape(2, nz, sub, tokens).transpose(1, 0, 2, 3)
        got = jnp.sum(exchange(packed, "zh").astype(F32), axis=0)
        back, tan_back = got[0], got[1]
        hv_down = dot(resid, tan_hidden, 1, 1) + dot(tan_resid, hidden, 1, 1)

        def deltas(tan_back, tan_gate, tan_upper):
            up = tan_back * activated + back * (slope_one * tan_gate)
            gate = (tan_back * upper + back * tan_upper) * slope_one + (
                back * upper
            ) * slope_two * tan_gate
            return jnp.concatenate([gate.astype(BF), up.astype(BF)])

        delta = deltas(tan_back, tan_gate, tan_upper)

        def lanes(v):
            v = jnp.sum(v, axis=0, keepdims=True)
            return jnp.pad(v, ((0, 0), (0, tokens - v.shape[1])))

        def terms(*values):
            return jnp.concatenate([t for v in values for t in two_terms(v)])

        tangents = by_gram(delta)
        square = lanes(delta.astype(F32) * tangents) + lanes(hv_down * hv_down)
        tan_gate, tan_upper = tangents[:sub], tangents[sub:]
        tan_hidden = ((slope_one * tan_gate) * upper + activated * tan_upper).astype(BF)
        both = gather(jnp.concatenate([tan_hidden, terms(square)]), "zh", nz)
        tan_hidden = both[:, :sub].reshape(ff, tokens)
        square = jnp.sum(both[:, sub:].astype(F32), axis=(0, 1))[None]

        hv_down_b = hv_down.astype(BF)
        tan_out = dot(down, tan_hidden, 1, 0) + dot(hv_down_b, hidden, 1, 0)
        packed = tan_out.astype(BF).reshape(nr, rows, 2, tokens // 2)
        scal = terms(square[:, : tokens // 2] + square[:, tokens // 2 :])
        scal = jnp.broadcast_to(scal[None, None], (nr, 1, 2, tokens // 2))
        got = exchange(jnp.concatenate([packed, scal], axis=1), REST)
        got, square = got[:, :rows].astype(F32), got[:, rows:].astype(F32)
        square = jnp.sum(square, axis=(0, 1, 2))[None]
        got = jnp.sum(got, axis=0).reshape(rows, tokens)
        scale = 1.0 / jnp.sqrt(total(square) / count + 1e-6)
        tan_resid = (got / tokens).astype(BF)
        tan_resid = gather(tan_resid, REST, nr).reshape(dz, tokens)

        tan_back = dot(down, tan_resid, 0, 0) + dot(hv_down_b, resid, 0, 0)
        packed = tan_back.astype(BF).reshape(nz, sub, tokens)
        tan_back = jnp.sum(exchange(packed, "zh").astype(F32), axis=0)
        hv_down2 = (dot(resid, tan_hidden, 1, 1) + dot(tan_resid, hidden, 1, 1)) * scale

        tangents = tangents * scale
        delta = deltas(tan_back * scale, tangents[:sub], tangents[sub:])
        wide = delta.astype(F32)
        inner = lanes(tangents * wide) + lanes((hv_down * scale) * hv_down2)
        square = lanes(by_gram(delta) * wide) + lanes(hv_down2 * hv_down2)
        both = gather(jnp.concatenate([delta, terms(inner, square)]), "zh", nz)
        delta_gate = both[:, :sub].reshape(ff, tokens)
        delta_up = both[:, sub : 2 * sub].reshape(ff, tokens)
        sums = both[:, 2 * sub :].reshape(nz, 2, 2, tokens).astype(F32)
        sums = jnp.sum(sums, axis=(0, 2))
        if tokens > LANES:
            sums = sums[:, :LANES] + sums[:, LANES:]
        sums = jnp.pad(sums, ((0, 0), (0, LANES - sums.shape[1])))
        sums = terms(sums)

        hv = [
            jnp.pad(v.reshape(nx, d_dev, ff), ((0, 0), (0, 0), (0, LANES - ff)))
            for v in (
                dot(inputs, delta_gate, 0, 1).astype(BF),
                dot(inputs, delta_up, 0, 1).astype(BF),
                hv_down2.astype(BF),
            )
        ]
        hv.append(jnp.broadcast_to(sums[None], (nx,) + sums.shape))
        got = exchange(jnp.concatenate(hv, axis=1), NEAR)
        sums = jnp.sum(got[:, 3 * d_dev :].astype(F32), axis=0)
        sums = jnp.sum(gather(sums[:2] + sums[2:], ("y", "core"), nt), axis=0)
        scale = 1.0 / jnp.sqrt(total(sums[1:]) / count + 1e-6)
        hv = got[:, : 3 * d_dev, :ff].reshape(nx, 3, d_dev, ff)
        hv = hv.transpose(1, 2, 0, 3).reshape(3, d_dev, ff_dev).astype(F32) * scale
        return hv[0], hv[1], hv[2].T, jnp.sum(sums[0]) / count

    return body


def build(devices, sizes):
    wide = Mesh(devices.reshape(sizes), AXES)
    dp, tensor = ("zh", *NEAR), ("y", "core")
    placed = (
        P(dp, tensor),
        P(dp),
        P(None, dp),
        P(dp, tensor),
        P(dp, tensor),
        P(tensor, dp),
        P(dp, tensor),
        P(dp, tensor),
        P(tensor, dp),
    )
    return jax.shard_map(
        make_body(*sizes),
        mesh=wide,
        in_specs=placed,
        out_specs=(P(dp, tensor), P(dp, tensor), P(tensor, dp), P()),
        check_vma=False,
    )


def solution(mesh):
    return build(mesh.devices, SIZES)
```

```python
import functools

import jax
import jax.numpy as jnp
from jax import lax
from jax.experimental import pallas as pl
from jax.experimental.pallas import tpu as pltpu
from jax.sharding import Mesh
from jax.sharding import PartitionSpec as P

AXES = ("zh", "zl", "x", "y", "core")
SIZES = (8, 2, 4, 4, 2)
NEAR = ("zl", "x")
REST = ("zl", "x", "y", "core")
LANES = 128
BF = jnp.bfloat16
F32 = jnp.float32


def dot(a, b, ca, cb):
    return lax.dot_general(a, b, (((ca,), (cb,)), ((), ())), preferred_element_type=F32)


def exchange(v, axes):
    return lax.all_to_all(v, axes, split_axis=0, concat_axis=0, tiled=True)


def gather(v, axes, n):
    return exchange(jnp.broadcast_to(v[None], (n,) + v.shape), axes)


def two_terms(v):
    high = lax.reduce_precision(v, 8, 7)
    return high.astype(BF), (v - high).astype(BF)


def silu_parts(values):
    s = jax.nn.sigmoid(values)
    activated = values * s
    slope_one = s * (1.0 + values * (1.0 - s))
    slope_two = s * (1.0 - s) * (2.0 + values * (1.0 - 2.0 * s))
    return activated, slope_one, slope_two


def total(v):
    ones = jnp.ones((v.shape[1], 128), F32)
    both = lax.dot_general(
        v, ones, (((1,), (0,)), ((), ())), precision=lax.Precision.HIGHEST, preferred_element_type=F32
    )
    return both[:, :1]


def pack_kernel(ff, *refs):
    out = refs[-1]
    for m, ref in enumerate(refs[:-1]):
        v = ref[...].astype(F32)
        for e in range(out.shape[0]):
            out[e, m] = v[:, e * ff : (e + 1) * ff].astype(BF)


def pack(mats, parts):
    rows, columns = mats[0].shape
    ff = columns // parts
    shape = (parts, len(mats), rows, ff)
    return pl.pallas_call(
        functools.partial(pack_kernel, ff),
        out_shape=jax.ShapeDtypeStruct(shape, BF),
        in_specs=[pl.BlockSpec(memory_space=pltpu.VMEM)] * len(mats),
        out_specs=pl.BlockSpec(memory_space=pltpu.VMEM),
        compiler_params=pltpu.CompilerParams(vmem_limit_bytes=16 << 20),
        cost_estimate=pl.CostEstimate(flops=0, bytes_accessed=2 << 20, transcendentals=0),
    )(*mats)


def make_body(nz, nl, nx, ny, nc):
    nt = ny * nc
    nx = nl * nx
    nr = nx * nt

    def body(pool, picks, targets, gate_w, up_w, down_w, probe_g, probe_u, probe_d):
        tok_dev = picks.shape[0]
        tokens = targets.shape[0]
        d_dev, ff_dev = gate_w.shape
        ff = ff_dev // nx
        dz = d_dev * nx
        sub = ff // nz
        rows = dz // nr
        count = 3.0 * (dz * nz) * (ff_dev * nt)

        picked = pool.at[picks].get(mode="promise_in_bounds")
        swap = [(i * nt + j, j * nz + i) for i in range(nz) for j in range(nt)]
        chosen = lax.ppermute(picked, ("zh", "y", "core"), swap)
        targets = targets.reshape(nz, nx, tok_dev, d_dev).transpose(1, 0, 2, 3)
        targets = targets.reshape(tokens, d_dev)

        mats = (gate_w, up_w, probe_g, probe_u, down_w.T, probe_d.T)
        picked, mats = lax.optimization_barrier((picked, mats))
        mats = pack(mats, nx)
        mats = exchange(mats, NEAR)
        chosen, mats = lax.optimization_barrier((chosen, mats))
        mats = mats.transpose(1, 0, 2, 3).reshape(6, dz, ff)
        inputs = gather(chosen, REST, nr).reshape(tokens, dz)
        down, pdown = mats[4], mats[5]

        first = lax.dot_general(
            mats[:4], inputs, (((1,), (1,)), ((), ())), preferred_element_type=F32
        )
        own = lax.axis_index(REST)
        gram_rows = tokens // nr
        mine = lax.dynamic_slice_in_dim(inputs, own * gram_rows, gram_rows, 0)
        gram = jnp.concatenate(two_terms(dot(mine, inputs, 1, 1)))
        packed = first.astype(BF).reshape(4, nz, sub, tokens).transpose(1, 0, 2, 3)
        packed = packed.reshape(nz, 4 * sub, tokens)
        packed = jnp.concatenate(
            [packed, jnp.broadcast_to(gram[None], (nz,) + gram.shape)], axis=1
        )
        got = jnp.sum(exchange(packed, "zh").astype(F32), axis=0)
        gate_val, upper, tan_gate, tan_upper = (
            got[i * sub : (i + 1) * sub] for i in range(4)
        )
        gram = got[4 * sub : 4 * sub + gram_rows] + got[4 * sub + gram_rows :]
        activated, slope_one, slope_two = silu_parts(gate_val)
        hidden = (activated * upper).astype(BF)
        tan_act = slope_one * tan_gate
        tan_hidden = (tan_act * upper + activated * tan_upper).astype(BF)
        both = gather(jnp.concatenate([hidden, tan_hidden]), "zh", nz)
        hidden = both[:, :sub].reshape(ff, tokens)
        tan_hidden = both[:, sub:].reshape(ff, tokens)

        out = dot(down, hidden, 1, 0)
        tan_out = dot(down, tan_hidden, 1, 0) + dot(pdown, hidden, 1, 0)
        packed = jnp.stack([out.astype(BF), tan_out.astype(BF)])
        packed = packed.reshape(2, nr, rows, tokens).transpose(1, 0, 2, 3)
        got = jnp.sum(exchange(packed, REST).astype(F32), axis=0)
        wanted = lax.dynamic_slice_in_dim(
            targets.T, lax.axis_index(("y", "core")) * rows, rows, 0
        )
        resid = ((got[0] - wanted.astype(F32)) / tokens).astype(BF)
        tan_resid = (got[1] / tokens).astype(BF)
        packed = jnp.concatenate([resid, tan_resid, *two_terms(gram)])
        both = gather(packed, REST, nr)
        resid = both[:, :rows].reshape(dz, tokens)
        tan_resid = both[:, rows : 2 * rows].reshape(dz, tokens)
        gram_hi = both[:, 2 * rows : 2 * rows + gram_rows].reshape(tokens, tokens)
        gram_lo = both[:, 2 * rows + gram_rows :].reshape(tokens, tokens)

        def by_gram(v):
            return dot(v, gram_hi, 1, 0) + dot(v, gram_lo, 1, 0)

        back = dot(down, resid, 0, 0)
        tan_back = dot(down, tan_resid, 0, 0) + dot(pdown, resid, 0, 0)
        packed = jnp.stack([back.astype(BF), tan_back.astype(BF)])
        packed = packed.reshape(2, nz, sub, tokens).transpose(1, 0, 2, 3)
        got = jnp.sum(exchange(packed, "zh").astype(F32), axis=0)
        back, tan_back = got[0], got[1]
        hv_down = dot(resid, tan_hidden, 1, 1) + dot(tan_resid, hidden, 1, 1)

        def deltas(tan_back, tan_gate, tan_upper):
            up = tan_back * activated + back * (slope_one * tan_gate)
            gate = (tan_back * upper + back * tan_upper) * slope_one + (
                back * upper
            ) * slope_two * tan_gate
            return jnp.concatenate([gate.astype(BF), up.astype(BF)])

        delta = deltas(tan_back, tan_gate, tan_upper)

        def lanes(v):
            v = jnp.sum(v, axis=0, keepdims=True)
            return jnp.pad(v, ((0, 0), (0, tokens - v.shape[1])))

        def terms(*values):
            return jnp.concatenate([t for v in values for t in two_terms(v)])

        tangents = by_gram(delta)
        square = lanes(delta.astype(F32) * tangents) + lanes(hv_down * hv_down)
        tan_gate, tan_upper = tangents[:sub], tangents[sub:]
        tan_hidden = ((slope_one * tan_gate) * upper + activated * tan_upper).astype(BF)
        both = gather(jnp.concatenate([tan_hidden, terms(square)]), "zh", nz)
        tan_hidden = both[:, :sub].reshape(ff, tokens)
        square = jnp.sum(both[:, sub:].astype(F32), axis=(0, 1))[None]

        hv_down_b = hv_down.astype(BF)
        tan_out = dot(down, tan_hidden, 1, 0) + dot(hv_down_b, hidden, 1, 0)
        packed = tan_out.astype(BF).reshape(nr, rows, 2, tokens // 2)
        scal = terms(square[:, : tokens // 2] + square[:, tokens // 2 :])
        scal = jnp.broadcast_to(scal[None, None], (nr, 1, 2, tokens // 2))
        got = exchange(jnp.concatenate([packed, scal], axis=1), REST)
        got, square = got[:, :rows].astype(F32), got[:, rows:].astype(F32)
        square = jnp.sum(square, axis=(0, 1, 2))[None]
        got = jnp.sum(got, axis=0).reshape(rows, tokens)
        scale = 1.0 / jnp.sqrt(total(square) / count + 1e-6)
        tan_resid = (got / tokens).astype(BF)
        tan_resid = gather(tan_resid, REST, nr).reshape(dz, tokens)

        tan_back = dot(down, tan_resid, 0, 0) + dot(hv_down_b, resid, 0, 0)
        packed = tan_back.astype(BF).reshape(nz, sub, tokens)
        tan_back = jnp.sum(exchange(packed, "zh").astype(F32), axis=0)
        hv_down2 = (dot(resid, tan_hidden, 1, 1) + dot(tan_resid, hidden, 1, 1)) * scale

        tangents = tangents * scale
        delta = deltas(tan_back * scale, tangents[:sub], tangents[sub:])
        wide = delta.astype(F32)
        inner = lanes(tangents * wide) + lanes((hv_down * scale) * hv_down2)
        square = lanes(by_gram(delta) * wide) + lanes(hv_down2 * hv_down2)
        both = gather(jnp.concatenate([delta, terms(inner, square)]), "zh", nz)
        delta_gate = both[:, :sub].reshape(ff, tokens)
        delta_up = both[:, sub : 2 * sub].reshape(ff, tokens)
        sums = both[:, 2 * sub :].reshape(nz, 2, 2, tokens).astype(F32)
        sums = jnp.sum(sums, axis=(0, 2))
        if tokens > LANES:
            sums = sums[:, :LANES] + sums[:, LANES:]
        sums = jnp.pad(sums, ((0, 0), (0, LANES - sums.shape[1])))
        sums = terms(sums)

        hv = [
            jnp.pad(v.reshape(nx, d_dev, ff), ((0, 0), (0, 0), (0, LANES - ff)))
            for v in (
                dot(inputs, delta_gate, 0, 1).astype(BF),
                dot(inputs, delta_up, 0, 1).astype(BF),
                hv_down2.astype(BF),
            )
        ]
        hv.append(jnp.broadcast_to(sums[None], (nx,) + sums.shape))
        got = exchange(jnp.concatenate(hv, axis=1), NEAR)
        sums = jnp.sum(got[:, 3 * d_dev :].astype(F32), axis=0)
        hv = got[:, : 3 * d_dev, :ff].reshape(nx, 3, d_dev, ff)
        hv = hv.transpose(1, 2, 0, 3).reshape(3, d_dev, ff_dev)
        sums = jnp.sum(gather(sums[:2] + sums[2:], ("y", "core"), nt), axis=0)
        hv, sums = lax.optimization_barrier((hv, sums))
        sums = total(sums)
        scale = 1.0 / jnp.sqrt(sums[1:] / count + 1e-6)
        gate, up, down = (v.astype(F32) * scale for v in hv)
        return gate, up, down.T, sums[0, 0] / count

    return body


def build(devices, sizes):
    wide = Mesh(devices.reshape(sizes), AXES)
    dp, tensor = ("zh", *NEAR), ("y", "core")
    placed = (
        P(dp, tensor),
        P(dp),
        P(None, dp),
        P(dp, tensor),
        P(dp, tensor),
        P(tensor, dp),
        P(dp, tensor),
        P(dp, tensor),
        P(tensor, dp),
    )
    return jax.shard_map(
        make_body(*sizes),
        mesh=wide,
        in_specs=placed,
        out_specs=(P(dp, tensor), P(dp, tensor), P(tensor, dp), P()),
        check_vma=False,
    )


def solution(mesh):
    return build(mesh.devices, SIZES)
```

```python
import functools

import jax
import jax.numpy as jnp
from jax import lax
from jax.experimental import pallas as pl
from jax.experimental.pallas import tpu as pltpu
from jax.sharding import Mesh
from jax.sharding import PartitionSpec as P

AXES = ("zh", "zl", "x", "y", "core")
SIZES = (8, 2, 4, 4, 2)
NEAR = ("zl", "x")
REST = ("zl", "x", "y", "core")
LANES = 128
BF = jnp.bfloat16
F32 = jnp.float32


def dot(a, b, ca, cb):
    return lax.dot_general(a, b, (((ca,), (cb,)), ((), ())), preferred_element_type=F32)


def exchange(v, axes):
    return lax.all_to_all(v, axes, split_axis=0, concat_axis=0, tiled=True)


def gather(v, axes, n):
    return exchange(jnp.broadcast_to(v[None], (n,) + v.shape), axes)


def two_terms(v):
    high = lax.reduce_precision(v, 8, 7)
    return high.astype(BF), (v - high).astype(BF)


def silu_parts(values):
    s = jax.nn.sigmoid(values)
    activated = values * s
    slope_one = s * (1.0 + values * (1.0 - s))
    slope_two = s * (1.0 - s) * (2.0 + values * (1.0 - 2.0 * s))
    return activated, slope_one, slope_two


def total(v):
    ones = jnp.ones((v.shape[1], LANES), F32)
    return lax.dot_general(
        v, ones, (((1,), (0,)), ((), ())), precision=lax.Precision.HIGHEST, preferred_element_type=F32
    )


def across(row, columns):
    return jnp.concatenate([row] * pl.cdiv(columns, LANES), axis=1)[:, :columns]


def pack_kernel(ff, count, *refs):
    mats, out, held, sem = refs[:count], refs[count], refs[count + 1 : -1], refs[-1]
    copies = [
        pltpu.make_async_copy(mats[m], held[m], sem.at[m]) for m in range(count)
    ]
    for copy in copies:
        copy.start()
    for m, copy in enumerate(copies):
        copy.wait()
        v = held[m][...].astype(F32)
        for e in range(out.shape[0]):
            out[e, m] = v[:, e * ff : (e + 1) * ff].astype(BF)


def pack(mats, parts):
    rows, columns = mats[0].shape
    ff = columns // parts
    shape = (parts, len(mats), rows, ff)
    return pl.pallas_call(
        functools.partial(pack_kernel, ff, len(mats)),
        out_shape=jax.ShapeDtypeStruct(shape, BF),
        in_specs=[pl.BlockSpec(memory_space=pl.ANY)] * len(mats),
        out_specs=pl.BlockSpec(memory_space=pltpu.VMEM),
        scratch_shapes=[pltpu.VMEM(m.shape, m.dtype) for m in mats]
        + [pltpu.SemaphoreType.DMA((len(mats),))],
        compiler_params=pltpu.CompilerParams(vmem_limit_bytes=56 << 20),
        cost_estimate=pl.CostEstimate(flops=0, bytes_accessed=2 << 20, transcendentals=0),
    )(*mats)


def make_body(nz, nl, nx, ny, nc):
    nt = ny * nc
    nx = nl * nx
    nr = nx * nt

    def body(pool, picks, targets, gate_w, up_w, down_w, probe_g, probe_u, probe_d):
        tok_dev = picks.shape[0]
        tokens = targets.shape[0]
        d_dev, ff_dev = gate_w.shape
        ff = ff_dev // nx
        dz = d_dev * nx
        sub = ff // nz
        rows = dz // nr
        count = 3.0 * (dz * nz) * (ff_dev * nt)

        picked = pool.at[picks].get(mode="promise_in_bounds")
        swap = [(i * nt + j, j * nz + i) for i in range(nz) for j in range(nt)]
        chosen = lax.ppermute(picked, ("zh", "y", "core"), swap)
        targets = targets.reshape(nz, nx, tok_dev, d_dev).transpose(1, 0, 2, 3)
        targets = targets.reshape(tokens, d_dev)

        mats = (gate_w, up_w, probe_g, probe_u, down_w.T, probe_d.T)
        picked, mats = lax.optimization_barrier((picked, mats))
        mats = pack(mats, nx)
        mats = exchange(mats, NEAR)
        chosen, mats = lax.optimization_barrier((chosen, mats))
        mats = mats.transpose(1, 0, 2, 3).reshape(6, dz, ff)
        inputs = gather(chosen, REST, nr).reshape(tokens, dz)
        down, pdown = mats[4], mats[5]

        def to_out(first, second):
            pair = jnp.concatenate([first, second], axis=1)
            return lambda h: dot(pair, h, 1, 0).astype(BF)

        def to_back(first, second):
            pair = jnp.concatenate([first, second], axis=0)
            return lambda r: dot(pair, r, 0, 0).astype(BF)

        def with_tangent(v, tan):
            upper = jnp.concatenate([v, tan], axis=1)
            lower = jnp.concatenate([jnp.zeros_like(v), v], axis=1)
            return jnp.concatenate([upper, lower], axis=0)

        first = lax.dot_general(
            mats[:4], inputs, (((1,), (1,)), ((), ())), preferred_element_type=F32
        )
        own = lax.axis_index(REST)
        gram_rows = tokens // nr
        mine = lax.dynamic_slice_in_dim(inputs, own * gram_rows, gram_rows, 0)
        gram = jnp.concatenate(two_terms(dot(mine, inputs, 1, 1)))
        packed = first.astype(BF).reshape(4, nz, sub, tokens).transpose(1, 0, 2, 3)
        packed = packed.reshape(nz, 4 * sub, tokens)
        packed = jnp.concatenate(
            [packed, jnp.broadcast_to(gram[None], (nz,) + gram.shape)], axis=1
        )
        got = jnp.sum(exchange(packed, "zh").astype(F32), axis=0)
        gate_val, upper, tan_gate, tan_upper = (
            got[i * sub : (i + 1) * sub] for i in range(4)
        )
        gram = got[4 * sub : 4 * sub + gram_rows] + got[4 * sub + gram_rows :]
        activated, slope_one, slope_two = silu_parts(gate_val)
        hidden = (activated * upper).astype(BF)
        tan_act = slope_one * tan_gate
        tan_hidden = (tan_act * upper + activated * tan_upper).astype(BF)
        both = gather(jnp.concatenate([hidden, tan_hidden]), "zh", nz)
        hidden = both[:, :sub].reshape(ff, tokens)
        tan_hidden = both[:, sub:].reshape(ff, tokens)

        packed = to_out(down, pdown)(with_tangent(hidden, tan_hidden))
        packed = packed.reshape(nr, rows, 2 * tokens)
        got = jnp.sum(exchange(packed, REST).astype(F32), axis=0)
        out, tan_out = got[:, :tokens], got[:, tokens:]
        wanted = lax.dynamic_slice_in_dim(
            targets.T, lax.axis_index(("y", "core")) * rows, rows, 0
        )
        resid = ((out - wanted.astype(F32)) / tokens).astype(BF)
        tan_resid = (tan_out / tokens).astype(BF)
        packed = jnp.concatenate([resid, tan_resid, *two_terms(gram)])
        both = gather(packed, REST, nr)
        resid = both[:, :rows].reshape(dz, tokens)
        tan_resid = both[:, rows : 2 * rows].reshape(dz, tokens)
        gram_hi = both[:, 2 * rows : 2 * rows + gram_rows].reshape(tokens, tokens)
        gram_lo = both[:, 2 * rows + gram_rows :].reshape(tokens, tokens)

        def by_gram(v):
            return dot(v, gram_hi, 1, 0) + dot(v, gram_lo, 1, 0)

        packed = to_back(down, pdown)(with_tangent(resid, tan_resid))
        packed = packed.reshape(nz, sub, 2 * tokens)
        got = jnp.sum(exchange(packed, "zh").astype(F32), axis=0)
        back, tan_back = got[:, :tokens], got[:, tokens:]
        hv_down = dot(resid, tan_hidden, 1, 1) + dot(tan_resid, hidden, 1, 1)

        def deltas(tan_back, tan_gate, tan_upper):
            up = tan_back * activated + back * (slope_one * tan_gate)
            gate = (tan_back * upper + back * tan_upper) * slope_one + (
                back * upper
            ) * slope_two * tan_gate
            return jnp.concatenate([gate.astype(BF), up.astype(BF)])

        delta = deltas(tan_back, tan_gate, tan_upper)

        def lanes(v):
            v = jnp.sum(v, axis=0, keepdims=True)
            return jnp.pad(v, ((0, 0), (0, tokens - v.shape[1])))

        def terms(*values):
            return jnp.concatenate([t for v in values for t in two_terms(v)])

        tangents = by_gram(delta)
        square = lanes(delta.astype(F32) * tangents) + lanes(hv_down * hv_down)
        tan_gate, tan_upper = tangents[:sub], tangents[sub:]
        tan_hidden = ((slope_one * tan_gate) * upper + activated * tan_upper).astype(BF)
        both = gather(jnp.concatenate([tan_hidden, terms(square)]), "zh", nz)
        tan_hidden = both[:, :sub].reshape(ff, tokens)
        square = jnp.sum(both[:, sub:].astype(F32), axis=(0, 1))[None]

        hv_down_b = hv_down.astype(BF)
        packed = to_out(down, hv_down_b)(jnp.concatenate([tan_hidden, hidden]))
        packed = packed.reshape(nr, rows, 2, tokens // 2)
        scal = terms(square[:, : tokens // 2] + square[:, tokens // 2 :])
        scal = jnp.broadcast_to(scal[None, None], (nr, 1, 2, tokens // 2))
        got = exchange(jnp.concatenate([packed, scal], axis=1), REST)
        got, square = got[:, :rows].astype(F32), got[:, rows:].astype(F32)
        square = jnp.sum(square, axis=(0, 1, 2))[None]
        got = jnp.sum(got, axis=0).reshape(rows, tokens)
        scale = 1.0 / jnp.sqrt(total(square) / count + 1e-6)
        tan_resid = (got / tokens).astype(BF)
        tan_resid = gather(tan_resid, REST, nr).reshape(dz, tokens)

        packed = to_back(down, hv_down_b)(jnp.concatenate([tan_resid, resid]))
        packed = packed.reshape(nz, sub, tokens)
        tan_back = jnp.sum(exchange(packed, "zh").astype(F32), axis=0)
        hv_down2 = (dot(resid, tan_hidden, 1, 1) + dot(tan_resid, hidden, 1, 1))
        hv_down2 = hv_down2 * across(scale, ff)
        wide_scale = across(scale, tokens)

        tangents = tangents * wide_scale
        delta = deltas(tan_back * wide_scale, tangents[:sub], tangents[sub:])
        wide = delta.astype(F32)
        inner = lanes(tangents * wide) + lanes((hv_down * across(scale, ff)) * hv_down2)
        square = lanes(by_gram(delta) * wide) + lanes(hv_down2 * hv_down2)
        both = gather(jnp.concatenate([delta, terms(inner, square)]), "zh", nz)
        delta_gate = both[:, :sub].reshape(ff, tokens)
        delta_up = both[:, sub : 2 * sub].reshape(ff, tokens)
        sums = both[:, 2 * sub :].reshape(nz, 2, 2, tokens).astype(F32)
        sums = jnp.sum(sums, axis=(0, 2))
        if tokens > LANES:
            sums = sums[:, :LANES] + sums[:, LANES:]
        sums = jnp.pad(sums, ((0, 0), (0, LANES - sums.shape[1])))
        sums = terms(sums)

        hv = [
            jnp.pad(v.reshape(nx, d_dev, ff), ((0, 0), (0, 0), (0, LANES - ff)))
            for v in (
                dot(inputs, delta_gate, 0, 1).astype(BF),
                dot(inputs, delta_up, 0, 1).astype(BF),
                hv_down2.astype(BF),
            )
        ]
        hv.append(jnp.broadcast_to(sums[None], (nx,) + sums.shape))
        got = exchange(jnp.concatenate(hv, axis=1), NEAR)
        sums = jnp.sum(got[:, 3 * d_dev :].astype(F32), axis=0)
        hv = got[:, : 3 * d_dev, :ff].reshape(nx, 3, d_dev, ff)
        hv = hv.transpose(1, 2, 0, 3).reshape(3, d_dev, ff_dev)
        sums = jnp.sum(gather(sums[:2] + sums[2:], ("y", "core"), nt), axis=0)
        hv, sums = lax.optimization_barrier((hv, sums))
        sums = total(sums)
        scale = across(1.0 / jnp.sqrt(sums[1:] / count + 1e-6), ff_dev)
        gate, up, down = (v.astype(F32) * scale for v in hv)
        return gate, up, down.T, sums[0, 0] / count

    return body


def build(devices, sizes):
    wide = Mesh(devices.reshape(sizes), AXES)
    dp, tensor = ("zh", *NEAR), ("y", "core")
    placed = (
        P(dp, tensor),
        P(dp),
        P(None, dp),
        P(dp, tensor),
        P(dp, tensor),
        P(tensor, dp),
        P(dp, tensor),
        P(dp, tensor),
        P(tensor, dp),
    )
    return jax.shard_map(
        make_body(*sizes),
        mesh=wide,
        in_specs=placed,
        out_specs=(P(dp, tensor), P(dp, tensor), P(tensor, dp), P()),
        check_vma=False,
    )


def solution(mesh):
    return build(mesh.devices, SIZES)
```

```python
import functools

import jax
import jax.numpy as jnp
from jax import lax
from jax.experimental import pallas as pl
from jax.experimental.pallas import tpu as pltpu
from jax.sharding import Mesh
from jax.sharding import PartitionSpec as P

AXES = ("zh", "zl", "x", "y", "core")
SIZES = (8, 2, 4, 4, 2)
NEAR = ("zl", "x")
REST = ("zl", "x", "y", "core")
LANES = 128
BF = jnp.bfloat16
F32 = jnp.float32


def dot(a, b, ca, cb):
    return lax.dot_general(a, b, (((ca,), (cb,)), ((), ())), preferred_element_type=F32)


def exchange(v, axes):
    return lax.all_to_all(v, axes, split_axis=0, concat_axis=0, tiled=True)


def alone(v, axes, live):
    v, live = lax.optimization_barrier((v, live))
    return lax.optimization_barrier((exchange(v, axes), live))


def gather(v, axes, n, live):
    return alone(jnp.broadcast_to(v[None], (n,) + v.shape), axes, live)


def two_terms(v):
    high = lax.reduce_precision(v, 8, 7)
    return high.astype(BF), (v - high).astype(BF)


def silu_parts(values):
    s = jax.nn.sigmoid(values)
    activated = values * s
    slope_one = s * (1.0 + values * (1.0 - s))
    slope_two = s * (1.0 - s) * (2.0 + values * (1.0 - 2.0 * s))
    return activated, slope_one, slope_two


def total(v):
    ones = jnp.ones((v.shape[1], LANES), F32)
    return lax.dot_general(
        v, ones, (((1,), (0,)), ((), ())), precision=lax.Precision.HIGHEST, preferred_element_type=F32
    )


def across(row, columns):
    return jnp.concatenate([row] * pl.cdiv(columns, LANES), axis=1)[:, :columns]


def pack_kernel(ff, count, *refs):
    mats, out, held, sem = refs[:count], refs[count], refs[count + 1 : -1], refs[-1]
    copies = [
        pltpu.make_async_copy(mats[m], held[m], sem.at[m]) for m in range(count)
    ]
    for copy in copies:
        copy.start()
    for m, copy in enumerate(copies):
        copy.wait()
        v = held[m][...].astype(F32)
        for e in range(out.shape[0]):
            out[e, m] = v[:, e * ff : (e + 1) * ff].astype(BF)


def pack(mats, parts):
    rows, columns = mats[0].shape
    ff = columns // parts
    shape = (parts, len(mats), rows, ff)
    return pl.pallas_call(
        functools.partial(pack_kernel, ff, len(mats)),
        out_shape=jax.ShapeDtypeStruct(shape, BF),
        in_specs=[pl.BlockSpec(memory_space=pl.ANY)] * len(mats),
        out_specs=pl.BlockSpec(memory_space=pltpu.VMEM),
        scratch_shapes=[pltpu.VMEM(m.shape, m.dtype) for m in mats]
        + [pltpu.SemaphoreType.DMA((len(mats),))],
        compiler_params=pltpu.CompilerParams(vmem_limit_bytes=56 << 20),
        cost_estimate=pl.CostEstimate(flops=0, bytes_accessed=2 << 20, transcendentals=0),
    )(*mats)


def make_body(nz, nl, nx, ny, nc):
    nt = ny * nc
    nx = nl * nx
    nr = nx * nt

    def body(pool, picks, targets, gate_w, up_w, down_w, probe_g, probe_u, probe_d):
        tok_dev = picks.shape[0]
        tokens = targets.shape[0]
        d_dev, ff_dev = gate_w.shape
        ff = ff_dev // nx
        dz = d_dev * nx
        sub = ff // nz
        rows = dz // nr
        count = 3.0 * (dz * nz) * (ff_dev * nt)

        picked = pool.at[picks].get(mode="promise_in_bounds")
        mats = (gate_w, up_w, probe_g, probe_u, down_w.T, probe_d.T)
        picked, mats = lax.optimization_barrier((picked, mats))
        swap = [(i * nt + j, j * nz + i) for i in range(nz) for j in range(nt)]
        chosen = lax.ppermute(picked, ("zh", "y", "core"), swap)
        mats = exchange(pack(mats, nx), NEAR)

        wanted = targets.reshape(nz, nx, tok_dev, d_dev).transpose(1, 0, 2, 3)
        wanted = wanted.reshape(tokens, d_dev).T
        wanted = lax.dynamic_slice_in_dim(
            wanted, lax.axis_index(("y", "core")) * rows, rows, 0
        )
        mats = mats.transpose(1, 0, 2, 3).reshape(6, dz, ff)
        live = {
            "own": lax.axis_index(REST),
            "wanted": wanted,
            "mats": mats[:4],
            "down": mats[4],
            "wide": jnp.concatenate([mats[4], mats[5]], axis=1),
            "tall": jnp.concatenate([mats[4], mats[5]], axis=0),
        }
        inputs, live = gather(chosen, REST, nr, live)
        inputs = live["inputs"] = inputs.reshape(tokens, dz)

        first = lax.dot_general(
            live.pop("mats"), inputs, (((1,), (1,)), ((), ())), preferred_element_type=F32
        )
        gram_rows = tokens // nr
        mine = lax.dynamic_slice_in_dim(inputs, live.pop("own") * gram_rows, gram_rows, 0)
        gram = jnp.concatenate(two_terms(dot(mine, inputs, 1, 1)))
        packed = first.astype(BF).reshape(4, nz, sub, tokens).transpose(1, 0, 2, 3)
        packed = packed.reshape(nz, 4 * sub, tokens)
        packed = jnp.concatenate(
            [packed, jnp.broadcast_to(gram[None], (nz,) + gram.shape)], axis=1
        )
        got, live = alone(packed, "zh", live)
        got = jnp.sum(got.astype(F32), axis=0)
        gate_val, upper, tan_gate, tan_upper = (
            got[i * sub : (i + 1) * sub] for i in range(4)
        )
        live["sums"] = (gate_val, upper, tan_gate, tan_upper)
        gram = got[4 * sub : 4 * sub + gram_rows] + got[4 * sub + gram_rows :]
        live["gram"] = jnp.concatenate(two_terms(gram))
        activated, slope_one, _ = silu_parts(gate_val)
        hidden = (activated * upper).astype(BF)
        tan_hidden = (slope_one * tan_gate * upper + activated * tan_upper).astype(BF)
        both, live = gather(jnp.concatenate([hidden, tan_hidden]), "zh", nz, live)
        hidden = live["hidden"] = both[:, :sub].reshape(ff, tokens)
        tan_hidden = live["tan_hidden"] = both[:, sub:].reshape(ff, tokens)

        def with_tangent(v, tan):
            upper = jnp.concatenate([v, tan], axis=1)
            lower = jnp.concatenate([jnp.zeros_like(v), v], axis=1)
            return jnp.concatenate([upper, lower], axis=0)

        out = dot(live.pop("wide"), with_tangent(hidden, tan_hidden), 1, 0).astype(BF)
        got, live = alone(out.reshape(nr, rows, 2 * tokens), REST, live)
        got = jnp.sum(got.astype(F32), axis=0)
        out, tan_out = got[:, :tokens], got[:, tokens:]
        resid = ((out - live.pop("wanted").astype(F32)) / tokens).astype(BF)
        tan_resid = (tan_out / tokens).astype(BF)
        packed = jnp.concatenate([resid, tan_resid, live.pop("gram")])
        both, live = gather(packed, REST, nr, live)
        resid = live["resid"] = both[:, :rows].reshape(dz, tokens)
        tan_resid = both[:, rows : 2 * rows].reshape(dz, tokens)
        gram_hi = both[:, 2 * rows : 2 * rows + gram_rows].reshape(tokens, tokens)
        gram_lo = both[:, 2 * rows + gram_rows :].reshape(tokens, tokens)
        live["gram"] = (gram_hi, gram_lo)

        back = dot(live.pop("tall"), with_tangent(resid, tan_resid), 0, 0).astype(BF)
        hv_down = dot(resid, live.pop("tan_hidden"), 1, 1)
        hv_down = live["hv_down"] = hv_down + dot(tan_resid, live["hidden"], 1, 1)
        down, hv_down_b = live.pop("down"), hv_down.astype(BF)
        live["wide"] = jnp.concatenate([down, hv_down_b], axis=1)
        live["tall"] = jnp.concatenate([down, hv_down_b], axis=0)

        def lanes(v):
            v = jnp.sum(v, axis=0, keepdims=True)
            return jnp.pad(v, ((0, 0), (0, tokens - v.shape[1])))

        def terms(*values):
            return jnp.concatenate([t for v in values for t in two_terms(v)])

        live["square"] = lanes(hv_down * hv_down)
        got, live = alone(back.reshape(nz, sub, 2 * tokens), "zh", live)
        got = jnp.sum(got.astype(F32), axis=0)
        live["back"] = got[:, :tokens]

        def by_gram(v):
            high, low = live["gram"]
            return dot(v, high, 1, 0) + dot(v, low, 1, 0)

        def deltas(tan_back, tan_gate, tan_upper):
            gate_val, upper, _, _ = live["sums"]
            activated, slope_one, slope_two = silu_parts(gate_val)
            back = live["back"]
            up = tan_back * activated + back * (slope_one * tan_gate)
            gate = (tan_back * upper + back * tan_upper) * slope_one + (
                back * upper
            ) * slope_two * tan_gate
            return jnp.concatenate([gate.astype(BF), up.astype(BF)])

        delta = deltas(got[:, tokens:], *live["sums"][2:])

        tangents = live["tangents"] = by_gram(delta)
        square = lanes(delta.astype(F32) * tangents) + live.pop("square")
        gate_val, upper, _, _ = live["sums"]
        activated, slope_one, _ = silu_parts(gate_val)
        tan_hidden = (
            (slope_one * tangents[:sub]) * upper + activated * tangents[sub:]
        ).astype(BF)
        both, live = gather(jnp.concatenate([tan_hidden, terms(square)]), "zh", nz, live)
        tan_hidden = live["tan_hidden"] = both[:, :sub].reshape(ff, tokens)
        square = jnp.sum(both[:, sub:].astype(F32), axis=(0, 1))[None]

        half = tokens // 2
        out = jnp.concatenate([tan_hidden, live["hidden"]])
        out = dot(live.pop("wide"), out, 1, 0).astype(BF).reshape(nr, rows, 2, half)
        scal = terms(square[:, :half] + square[:, half:])
        scal = jnp.broadcast_to(scal[None, None], (nr, 1, 2, half))
        got, live = alone(jnp.concatenate([out, scal], axis=1), REST, live)
        got, square = got[:, :rows].astype(F32), got[:, rows:].astype(F32)
        square = jnp.sum(square, axis=(0, 1, 2))[None]
        live["scale"] = 1.0 / jnp.sqrt(total(square) / count + 1e-6)
        got = jnp.sum(got, axis=0).reshape(rows, tokens)
        tan_resid = (got / tokens).astype(BF)
        tan_resid, live = gather(tan_resid, REST, nr, live)
        tan_resid = tan_resid.reshape(dz, tokens)

        resid = live.pop("resid")
        back = dot(live.pop("tall"), jnp.concatenate([tan_resid, resid]), 0, 0).astype(BF)
        scale = live.pop("scale")
        hv_down2 = dot(resid, live.pop("tan_hidden"), 1, 1)
        hv_down2 = hv_down2 + dot(tan_resid, live.pop("hidden"), 1, 1)
        hv_down2 = hv_down2 * across(scale, ff)
        live["inner"] = lanes((live.pop("hv_down") * across(scale, ff)) * hv_down2)
        live["square"] = lanes(hv_down2 * hv_down2)
        live["hv_down"] = hv_down2.astype(BF)
        live["scale"] = across(scale, tokens)
        got, live = alone(back.reshape(nz, sub, tokens), "zh", live)
        got = jnp.sum(got.astype(F32), axis=0)

        scale = live.pop("scale")
        tangents = live.pop("tangents") * scale
        delta = deltas(got * scale, tangents[:sub], tangents[sub:])
        wide = delta.astype(F32)
        inner = lanes(tangents * wide) + live.pop("inner")
        square = lanes(by_gram(delta) * wide) + live.pop("square")
        del live["gram"], live["sums"], live["back"]
        both, live = gather(jnp.concatenate([delta, terms(inner, square)]), "zh", nz, live)
        delta_gate = both[:, :sub].reshape(ff, tokens)
        delta_up = both[:, sub : 2 * sub].reshape(ff, tokens)
        sums = both[:, 2 * sub :].reshape(nz, 2, 2, tokens).astype(F32)
        sums = jnp.sum(sums, axis=(0, 2))
        if tokens > LANES:
            sums = sums[:, :LANES] + sums[:, LANES:]
        sums = jnp.pad(sums, ((0, 0), (0, LANES - sums.shape[1])))
        sums = terms(sums)

        hv = [
            jnp.pad(v.reshape(nx, d_dev, ff), ((0, 0), (0, 0), (0, LANES - ff)))
            for v in (
                dot(live["inputs"], delta_gate, 0, 1).astype(BF),
                dot(live["inputs"], delta_up, 0, 1).astype(BF),
                live["hv_down"],
            )
        ]
        hv.append(jnp.broadcast_to(sums[None], (nx,) + sums.shape))
        got, _ = alone(jnp.concatenate(hv, axis=1), NEAR, ())
        sums = jnp.sum(got[:, 3 * d_dev :].astype(F32), axis=0)
        hv = got[:, : 3 * d_dev, :ff].reshape(nx, 3, d_dev, ff)
        hv = hv.transpose(1, 2, 0, 3).reshape(3, d_dev, ff_dev)
        sums, hv = gather(sums[:2] + sums[2:], ("y", "core"), nt, hv)
        sums = total(jnp.sum(sums, axis=0))
        scale = across(1.0 / jnp.sqrt(sums[1:] / count + 1e-6), ff_dev)
        gate, up, down = (v.astype(F32) * scale for v in hv)
        return gate, up, down.T, sums[0, 0] / count

    return body


def build(devices, sizes):
    wide = Mesh(devices.reshape(sizes), AXES)
    dp, tensor = ("zh", *NEAR), ("y", "core")
    placed = (
        P(dp, tensor),
        P(dp),
        P(None, dp),
        P(dp, tensor),
        P(dp, tensor),
        P(tensor, dp),
        P(dp, tensor),
        P(dp, tensor),
        P(tensor, dp),
    )
    return jax.shard_map(
        make_body(*sizes),
        mesh=wide,
        in_specs=placed,
        out_specs=(P(dp, tensor), P(dp, tensor), P(tensor, dp), P()),
        check_vma=False,
    )


def solution(mesh):
    return build(mesh.devices, SIZES)
```

```python
import functools

import jax
import jax.numpy as jnp
from jax import lax
from jax.experimental import pallas as pl
from jax.experimental.pallas import tpu as pltpu
from jax.sharding import Mesh
from jax.sharding import PartitionSpec as P

AXES = ("zh", "zl", "x", "y", "core")
SIZES = (8, 2, 4, 4, 2)
NEAR = ("zl", "x")
REST = ("zl", "x", "y", "core")
QUAD = ("zl", "x", "y")
LANES = 128
BF = jnp.bfloat16
F32 = jnp.float32


def dot(a, b, ca, cb):
    return lax.dot_general(a, b, (((ca,), (cb,)), ((), ())), preferred_element_type=F32)


def exchange(v, axes):
    return lax.all_to_all(v, axes, split_axis=0, concat_axis=0, tiled=True)


def alone(v, axes, live):
    v, live = lax.optimization_barrier((v, live))
    return lax.optimization_barrier((exchange(v, axes), live))


def gather(v, axes, n, live):
    return alone(jnp.broadcast_to(v[None], (n,) + v.shape), axes, live)


def two_terms(v):
    high = lax.reduce_precision(v, 8, 7)
    return high.astype(BF), (v - high).astype(BF)


def sibling(v):
    return lax.ppermute(v, "core", [(0, 1), (1, 0)])


def silu_parts(values):
    s = jax.nn.sigmoid(values)
    activated = values * s
    slope_one = s * (1.0 + values * (1.0 - s))
    slope_two = s * (1.0 - s) * (2.0 + values * (1.0 - 2.0 * s))
    return activated, slope_one, slope_two


def total(v):
    ones = jnp.ones((v.shape[1], LANES), F32)
    return lax.dot_general(
        v, ones, (((1,), (0,)), ((), ())), precision=lax.Precision.HIGHEST, preferred_element_type=F32
    )


def across(row, columns):
    return jnp.concatenate([row] * pl.cdiv(columns, LANES), axis=1)[:, :columns]


def pack_kernel(ff, count, *refs):
    mats, out, held, sem = refs[:count], refs[count], refs[count + 1 : -1], refs[-1]
    copies = [
        pltpu.make_async_copy(mats[m], held[m], sem.at[m]) for m in range(count)
    ]
    for copy in copies:
        copy.start()
    for m, copy in enumerate(copies):
        copy.wait()
        v = held[m][...].astype(F32)
        for e in range(out.shape[0]):
            out[e, m] = v[:, e * ff : (e + 1) * ff].astype(BF)


def pack(mats, parts):
    rows, columns = mats[0].shape
    ff = columns // parts
    shape = (parts, len(mats), rows, ff)
    return pl.pallas_call(
        functools.partial(pack_kernel, ff, len(mats)),
        out_shape=jax.ShapeDtypeStruct(shape, BF),
        in_specs=[pl.BlockSpec(memory_space=pl.ANY)] * len(mats),
        out_specs=pl.BlockSpec(memory_space=pltpu.VMEM),
        scratch_shapes=[pltpu.VMEM(m.shape, m.dtype) for m in mats]
        + [pltpu.SemaphoreType.DMA((len(mats),))],
        compiler_params=pltpu.CompilerParams(vmem_limit_bytes=56 << 20),
        cost_estimate=pl.CostEstimate(flops=0, bytes_accessed=2 << 20, transcendentals=0),
    )(*mats)


def make_body(nz, nl, nx, ny, nc):
    nt = ny * nc
    nx = nl * nx
    nr = nx * nt

    def body(pool, picks, targets, gate_w, up_w, down_w, probe_g, probe_u, probe_d):
        tok_dev = picks.shape[0]
        tokens = targets.shape[0]
        d_dev, ff_dev = gate_w.shape
        ff = ff_dev // nx
        dz = d_dev * nx
        sub = ff // nz
        rows = dz // nr
        nq = nr // nc
        part = dz // nc
        core = lax.axis_index("core")
        count = 3.0 * (dz * nz) * (ff_dev * nt)

        picked = pool.at[picks].get(mode="promise_in_bounds")
        mats = (gate_w, up_w, probe_g, probe_u, down_w.T, probe_d.T)
        picked, mats = lax.optimization_barrier((picked, mats))
        swap = [(i * nt + j, j * nz + i) for i in range(nz) for j in range(nt)]
        chosen = lax.ppermute(picked, ("zh", "y", "core"), swap)
        mats = exchange(pack(mats, nx), NEAR)

        wanted = targets.reshape(nz, nx, tok_dev, d_dev).transpose(1, 0, 2, 3)
        wanted = wanted.reshape(tokens, d_dev).T
        wanted = lax.dynamic_slice_in_dim(
            wanted, lax.axis_index(("y", "core")) * rows, rows, 0
        )
        mats = mats.transpose(1, 0, 2, 3)

        def halves(v):
            mine = lax.dynamic_index_in_dim(v, core, 0, keepdims=False)
            return mine, lax.dynamic_index_in_dim(v, 1 - core, 0, keepdims=False)

        pair = mats[4:].reshape(2, nx, ny, nc, rows, ff).transpose(3, 0, 1, 2, 4, 5)
        mine, other = halves(pair.reshape(nc, 2, part, ff))
        live = {
            "own": core * nq + lax.axis_index(QUAD),
            "first": core == 0,
            "wanted": wanted,
            "mats": mats[:4].reshape(4, dz, ff),
            "down": jnp.concatenate([mine[0], other[0]], axis=0),
            "wide": jnp.concatenate([mine[0], mine[1]], axis=1),
            "away": jnp.concatenate([other[0], other[1]], axis=1),
            "tall": jnp.concatenate([mine[0], other[0], mine[1], other[1]], axis=0),
        }
        inputs, live = gather(chosen, REST, nr, live)
        inputs = live["inputs"] = inputs.reshape(tokens, dz)

        first = lax.dot_general(
            live.pop("mats"), inputs, (((1,), (1,)), ((), ())), preferred_element_type=F32
        )
        gram_rows = tokens // nr
        mine = lax.dynamic_slice_in_dim(inputs, live.pop("own") * gram_rows, gram_rows, 0)
        gram = jnp.concatenate(two_terms(dot(mine, inputs, 1, 1)))
        packed = first.astype(BF).reshape(4, nz, sub, tokens).transpose(1, 0, 2, 3)
        packed = packed.reshape(nz, 4 * sub, tokens)
        packed = jnp.concatenate(
            [packed, jnp.broadcast_to(gram[None], (nz,) + gram.shape)], axis=1
        )
        got, live = alone(packed, "zh", live)
        got = jnp.sum(got.astype(F32), axis=0)
        gate_val, upper, tan_gate, tan_upper = (
            got[i * sub : (i + 1) * sub] for i in range(4)
        )
        live["sums"] = (gate_val, upper, tan_gate, tan_upper)
        gram = got[4 * sub : 4 * sub + gram_rows] + got[4 * sub + gram_rows :]
        live["gram"] = jnp.concatenate(two_terms(gram))
        activated, slope_one, _ = silu_parts(gate_val)
        hidden = (activated * upper).astype(BF)
        tan_hidden = (slope_one * tan_gate * upper + activated * tan_upper).astype(BF)
        both, live = gather(jnp.concatenate([hidden, tan_hidden]), "zh", nz, live)
        hidden = live["hidden"] = both[:, :sub].reshape(ff, tokens)
        tan_hidden = live["tan_hidden"] = both[:, sub:].reshape(ff, tokens)

        def with_tangent(v, tan):
            upper = jnp.concatenate([v, tan], axis=1)
            lower = jnp.concatenate([jnp.zeros_like(v), v], axis=1)
            return jnp.concatenate([upper, lower], axis=0)

        both = with_tangent(hidden, tan_hidden)
        got = sibling(dot(live.pop("away"), both, 1, 0).astype(BF))
        out = (dot(live.pop("wide"), both, 1, 0) + got.astype(F32)).astype(BF)
        got, live = alone(out.reshape(nq, rows, 2 * tokens), QUAD, live)
        got = jnp.sum(got.astype(F32), axis=0)
        out, tan_out = got[:, :tokens], got[:, tokens:]
        resid = ((out - live.pop("wanted").astype(F32)) / tokens).astype(BF)
        tan_resid = (tan_out / tokens).astype(BF)
        packed = jnp.concatenate([resid, tan_resid, live.pop("gram")])
        mine, live = gather(packed, QUAD, nq, live)
        other = sibling(mine)

        def joined(start, stop):
            each = (v[:, start:stop].reshape(nq * (stop - start), tokens) for v in (mine, other))
            return jnp.concatenate(list(each), axis=0)

        def in_order(v):
            swapped = jnp.concatenate([v[tokens // 2 :], v[: tokens // 2]], axis=0)
            return jnp.where(live["first"], v, swapped)

        resid = live["resid"] = joined(0, rows)
        tan_resid = joined(rows, 2 * rows)
        live["gram"] = (
            in_order(joined(2 * rows, 2 * rows + gram_rows)),
            in_order(joined(2 * rows + gram_rows, 2 * rows + 2 * gram_rows)),
        )

        del live["first"]

        back = dot(live.pop("tall"), with_tangent(resid, tan_resid), 0, 0).astype(BF)
        hv_down = dot(resid, live.pop("tan_hidden"), 1, 1)
        hv_down = live["hv_down"] = hv_down + dot(tan_resid, live["hidden"], 1, 1)
        live["hv_down_b"] = hv_down.astype(BF)

        def lanes(v):
            v = jnp.sum(v, axis=0, keepdims=True)
            return jnp.pad(v, ((0, 0), (0, tokens - v.shape[1])))

        def terms(*values):
            return jnp.concatenate([t for v in values for t in two_terms(v)])

        live["square"] = lanes(hv_down * hv_down)
        got, live = alone(back.reshape(nz, sub, 2 * tokens), "zh", live)
        got = jnp.sum(got.astype(F32), axis=0)
        live["back"] = got[:, :tokens]

        def by_gram(v):
            high, low = live["gram"]
            return dot(v, high, 1, 0) + dot(v, low, 1, 0)

        def deltas(tan_back, tan_gate, tan_upper):
            gate_val, upper, _, _ = live["sums"]
            activated, slope_one, slope_two = silu_parts(gate_val)
            back = live["back"]
            up = tan_back * activated + back * (slope_one * tan_gate)
            gate = (tan_back * upper + back * tan_upper) * slope_one + (
                back * upper
            ) * slope_two * tan_gate
            return jnp.concatenate([gate.astype(BF), up.astype(BF)])

        delta = deltas(got[:, tokens:], *live["sums"][2:])

        tangents = live["tangents"] = by_gram(delta)
        square = lanes(delta.astype(F32) * tangents) + live.pop("square")
        gate_val, upper, _, _ = live["sums"]
        activated, slope_one, _ = silu_parts(gate_val)
        tan_hidden = (
            (slope_one * tangents[:sub]) * upper + activated * tangents[sub:]
        ).astype(BF)
        both, live = gather(jnp.concatenate([tan_hidden, terms(square)]), "zh", nz, live)
        tan_hidden = live["tan_hidden"] = both[:, :sub].reshape(ff, tokens)
        square = jnp.sum(both[:, sub:].astype(F32), axis=(0, 1))[None]

        def out_rows(start, stop):
            v = dot(live["down"][start:stop], tan_hidden, 1, 0)
            return v + dot(live["hv_down_b"][start:stop], live["hidden"], 1, 0)

        half = tokens // 2
        got = jnp.concatenate([out_rows(part, dz).astype(BF), terms(square)])
        got = sibling(got).astype(F32)
        out = (out_rows(0, part) + got[:part]).astype(BF).reshape(nq, rows, 2, half)
        square = square + got[part : part + 1] + got[part + 1 :]
        scal = terms(square[:, :half] + square[:, half:])
        scal = jnp.broadcast_to(scal[None, None], (nq, 1, 2, half))
        got, live = alone(jnp.concatenate([out, scal], axis=1), QUAD, live)
        got, square = got[:, :rows].astype(F32), got[:, rows:].astype(F32)
        square = jnp.sum(square, axis=(0, 1, 2))[None]
        live["scale"] = 1.0 / jnp.sqrt(total(square) / count + 1e-6)
        got = jnp.sum(got, axis=0).reshape(rows, tokens)
        tan_resid = (got / tokens).astype(BF)
        tan_resid, live = gather(tan_resid, QUAD, nq, live)
        tan_resid = tan_resid.reshape(part, tokens)
        tan_resid = jnp.concatenate([tan_resid, sibling(tan_resid)], axis=0)

        resid = live.pop("resid")
        back = dot(live.pop("down"), tan_resid, 0, 0)
        back = (back + dot(live.pop("hv_down_b"), resid, 0, 0)).astype(BF)
        scale = live.pop("scale")
        hv_down2 = dot(resid, live.pop("tan_hidden"), 1, 1)
        hv_down2 = hv_down2 + dot(tan_resid, live.pop("hidden"), 1, 1)
        hv_down2 = hv_down2 * across(scale, ff)
        live["inner"] = lanes((live.pop("hv_down") * across(scale, ff)) * hv_down2)
        live["square"] = lanes(hv_down2 * hv_down2)
        hv_down2 = jnp.stack(halves(hv_down2.astype(BF).reshape(nc, part, ff)))
        hv_down2 = hv_down2.reshape(nc, nx, ny, rows, ff).transpose(1, 2, 0, 3, 4)
        live["hv_down"] = hv_down2.reshape(dz, ff)
        live["scale"] = across(scale, tokens)
        got, live = alone(back.reshape(nz, sub, tokens), "zh", live)
        got = jnp.sum(got.astype(F32), axis=0)

        scale = live.pop("scale")
        tangents = live.pop("tangents") * scale
        delta = deltas(got * scale, tangents[:sub], tangents[sub:])
        wide = delta.astype(F32)
        inner = lanes(tangents * wide) + live.pop("inner")
        square = lanes(by_gram(delta) * wide) + live.pop("square")
        del live["gram"], live["sums"], live["back"]
        both, live = gather(jnp.concatenate([delta, terms(inner, square)]), "zh", nz, live)
        delta_gate = both[:, :sub].reshape(ff, tokens)
        delta_up = both[:, sub : 2 * sub].reshape(ff, tokens)
        sums = both[:, 2 * sub :].reshape(nz, 2, 2, tokens).astype(F32)
        sums = jnp.sum(sums, axis=(0, 2))
        if tokens > LANES:
            sums = sums[:, :LANES] + sums[:, LANES:]
        sums = jnp.pad(sums, ((0, 0), (0, LANES - sums.shape[1])))
        sums = terms(sums)

        hv = [
            jnp.pad(v.reshape(nx, d_dev, ff), ((0, 0), (0, 0), (0, LANES - ff)))
            for v in (
                dot(live["inputs"], delta_gate, 0, 1).astype(BF),
                dot(live["inputs"], delta_up, 0, 1).astype(BF),
                live["hv_down"],
            )
        ]
        hv.append(jnp.broadcast_to(sums[None], (nx,) + sums.shape))
        got, _ = alone(jnp.concatenate(hv, axis=1), NEAR, ())
        sums = jnp.sum(got[:, 3 * d_dev :].astype(F32), axis=0)
        hv = got[:, : 3 * d_dev, :ff].reshape(nx, 3, d_dev, ff)
        hv = hv.transpose(1, 2, 0, 3).reshape(3, d_dev, ff_dev)
        sums, hv = gather(sums[:2] + sums[2:], ("y", "core"), nt, hv)
        sums = total(jnp.sum(sums, axis=0))
        scale = across(1.0 / jnp.sqrt(sums[1:] / count + 1e-6), ff_dev)
        gate, up, down = (v.astype(F32) * scale for v in hv)
        return gate, up, down.T, sums[0, 0] / count

    return body


def build(devices, sizes):
    wide = Mesh(devices.reshape(sizes), AXES)
    dp, tensor = ("zh", *NEAR), ("y", "core")
    placed = (
        P(dp, tensor),
        P(dp),
        P(None, dp),
        P(dp, tensor),
        P(dp, tensor),
        P(tensor, dp),
        P(dp, tensor),
        P(dp, tensor),
        P(tensor, dp),
    )
    return jax.shard_map(
        make_body(*sizes),
        mesh=wide,
        in_specs=placed,
        out_specs=(P(dp, tensor), P(dp, tensor), P(tensor, dp), P()),
        check_vma=False,
    )


def solution(mesh):
    return build(mesh.devices, SIZES)
```

```python
import functools

import jax
import jax.numpy as jnp
from jax import lax
from jax.experimental import pallas as pl
from jax.experimental.pallas import tpu as pltpu
from jax.sharding import Mesh
from jax.sharding import PartitionSpec as P

AXES = ("zh", "zl", "x", "y", "core")
SIZES = (8, 2, 4, 4, 2)
NEAR = ("zl", "x")
REST = ("zl", "x", "y", "core")
QUAD = ("zl", "x", "y")
LANES = 128
TILE = 16
BF = jnp.bfloat16
F32 = jnp.float32


def dot(a, b, ca, cb):
    return lax.dot_general(a, b, (((ca,), (cb,)), ((), ())), preferred_element_type=F32)


def exchange(v, axes):
    return lax.all_to_all(v, axes, split_axis=0, concat_axis=0, tiled=True)


def alone(v, axes, live):
    v, live = lax.optimization_barrier((v, live))
    return lax.optimization_barrier((exchange(v, axes), live))


def gather(v, axes, n, live):
    return alone(jnp.broadcast_to(v[None], (n,) + v.shape), axes, live)


def two_terms(v):
    high = lax.reduce_precision(v, 8, 7)
    return high.astype(BF), (v - high).astype(BF)


def sibling(v):
    return lax.ppermute(v, "core", [(0, 1), (1, 0)])


def silu_parts(values):
    s = jax.nn.sigmoid(values)
    activated = values * s
    slope_one = s * (1.0 + values * (1.0 - s))
    slope_two = s * (1.0 - s) * (2.0 + values * (1.0 - 2.0 * s))
    return activated, slope_one, slope_two


def total(v, columns):
    ones = jnp.ones((v.shape[1], columns), F32)
    return lax.dot_general(
        v, ones, (((1,), (0,)), ((), ())), precision=lax.Precision.HIGHEST, preferred_element_type=F32
    )


def load_kernel(ff, count, picks, pool, *refs):
    mats, chosen, out = refs[:count], refs[count], refs[count + 1]
    held, near, sem = refs[count + 2 : -2], refs[-2], refs[-1]
    tok_dev = chosen.shape[0]
    copies = []
    for k in range(tok_dev):
        first = pl.multiple_of(picks[k] // TILE * TILE, TILE)
        copies.append(
            pltpu.make_async_copy(pool.at[pl.ds(first, TILE)], near.at[k], sem.at[count + k])
        )
    for m in range(count):
        copies.append(pltpu.make_async_copy(mats[m], held[m], sem.at[m]))
    for copy in copies:
        copy.start()
    for m in range(count):
        copies[tok_dev + m].wait()
        v = held[m][...].astype(F32)
        for e in range(out.shape[0]):
            out[e, m] = v[:, e * ff : (e + 1) * ff].astype(BF)
    picked = []
    for k in range(tok_dev):
        copies[k].wait()
        v = near[k].astype(F32)
        row = lax.broadcasted_iota(jnp.int32, v.shape, 0)
        v = jnp.where(row == picks[k] % TILE, v, 0.0)
        picked.append(jnp.sum(v, axis=0, keepdims=True))
    chosen[...] = jnp.concatenate(picked, axis=0).astype(BF)


def load(picks, pool, mats, parts):
    rows, columns = mats[0].shape
    ff = columns // parts
    tok_dev, width = picks.shape[0], pool.shape[1]
    return pl.pallas_call(
        functools.partial(load_kernel, ff, len(mats)),
        out_shape=[
            jax.ShapeDtypeStruct((tok_dev, width), BF),
            jax.ShapeDtypeStruct((parts, len(mats), rows, ff), BF),
        ],
        in_specs=[pl.BlockSpec(memory_space=pltpu.SMEM)]
        + [pl.BlockSpec(memory_space=pl.ANY)] * (1 + len(mats)),
        out_specs=[pl.BlockSpec(memory_space=pltpu.VMEM)] * 2,
        scratch_shapes=[pltpu.VMEM(m.shape, m.dtype) for m in mats]
        + [
            pltpu.VMEM((tok_dev, TILE, width), BF),
            pltpu.SemaphoreType.DMA((len(mats) + tok_dev,)),
        ],
        compiler_params=pltpu.CompilerParams(vmem_limit_bytes=56 << 20),
        cost_estimate=pl.CostEstimate(flops=0, bytes_accessed=2 << 20, transcendentals=0),
    )(picks, pool, *mats)


def make_body(nz, nl, nx, ny, nc):
    nt = ny * nc
    nx = nl * nx
    nr = nx * nt

    def body(pool, picks, targets, gate_w, up_w, down_w, probe_g, probe_u, probe_d):
        tok_dev = picks.shape[0]
        tokens = targets.shape[0]
        d_dev, ff_dev = gate_w.shape
        ff = ff_dev // nx
        dz = d_dev * nx
        sub = ff // nz
        rows = dz // nr
        nq = nr // nc
        count = 3.0 * (dz * nz) * (ff_dev * nt)

        mats = (gate_w, up_w, probe_g, probe_u, down_w.T, probe_d.T)
        picked, mats = load(picks, pool, mats, nx)
        swap = [(i * nt + j, j * nz + i) for i in range(nz) for j in range(nt)]
        chosen = lax.ppermute(picked, ("zh", "y", "core"), swap)
        mats = exchange(mats, NEAR)

        wanted = targets.reshape(nz, nx, tok_dev, d_dev).transpose(1, 0, 2, 3)
        wanted = wanted.reshape(tokens, d_dev).T
        wanted = lax.dynamic_slice_in_dim(
            wanted, lax.axis_index(("y", "core")) * rows, rows, 0
        )
        mats = mats.transpose(1, 0, 2, 3).reshape(6, dz, ff)
        live = {
            "own": lax.axis_index(REST),
            "wanted": wanted,
            "mats": mats[:4],
            "first": lax.axis_index("core") == 0,
            "down": mats[4],
            "wide": jnp.concatenate([mats[4], mats[5]], axis=1),
            "tall": mats[4:].reshape(2 * dz, ff),
        }
        inputs, live = gather(chosen, REST, nr, live)
        inputs = live["inputs"] = inputs.reshape(tokens, dz)

        first = lax.dot_general(
            live.pop("mats"), inputs, (((1,), (1,)), ((), ())), preferred_element_type=F32
        )
        gram_rows = tokens // nr
        mine = lax.dynamic_slice_in_dim(inputs, live.pop("own") * gram_rows, gram_rows, 0)
        gram = jnp.concatenate(two_terms(dot(mine, inputs, 1, 1)))
        packed = first.astype(BF).reshape(4, nz, sub, tokens).transpose(1, 0, 2, 3)
        packed = packed.reshape(nz, 4 * sub, tokens)
        packed = jnp.concatenate(
            [packed, jnp.broadcast_to(gram[None], (nz,) + gram.shape)], axis=1
        )
        got, live = alone(packed, "zh", live)
        got = jnp.sum(got.astype(F32), axis=0)
        gate_val, upper, tan_gate, tan_upper = (
            got[i * sub : (i + 1) * sub] for i in range(4)
        )
        live["sums"] = (gate_val, upper, tan_gate, tan_upper)
        gram = got[4 * sub : 4 * sub + gram_rows] + got[4 * sub + gram_rows :]
        live["gram"] = jnp.concatenate(two_terms(gram))
        activated, slope_one, _ = silu_parts(gate_val)
        hidden = (activated * upper).astype(BF)
        tan_hidden = (slope_one * tan_gate * upper + activated * tan_upper).astype(BF)
        both, live = gather(jnp.concatenate([hidden, tan_hidden]), "zh", nz, live)
        hidden = live["hidden"] = both[:, :sub].reshape(ff, tokens)
        tan_hidden = live["tan_hidden"] = both[:, sub:].reshape(ff, tokens)

        def with_tangent(v, tan):
            upper = jnp.concatenate([v, tan], axis=1)
            lower = jnp.concatenate([jnp.zeros_like(v), v], axis=1)
            return jnp.concatenate([upper, lower], axis=0)

        out = dot(live.pop("wide"), with_tangent(hidden, tan_hidden), 1, 0).astype(BF)
        got, live = alone(out.reshape(nr, rows, 2 * tokens), REST, live)
        got = jnp.sum(got.astype(F32), axis=0)
        out, tan_out = got[:, :tokens], got[:, tokens:]
        resid = ((out - live.pop("wanted").astype(F32)) / tokens).astype(BF)
        tan_resid = (tan_out / tokens).astype(BF)
        packed = jnp.concatenate([resid, tan_resid, live.pop("gram")])
        mine, live = gather(packed, QUAD, nq, live)
        other, first = sibling(mine), live.pop("first")
        both = jnp.stack([jnp.where(first, mine, other), jnp.where(first, other, mine)], axis=1)

        def joined(start, stop):
            return both[:, :, start:stop].reshape(nr * (stop - start), tokens)

        resid = live["resid"] = joined(0, rows)
        tan_resid = joined(rows, 2 * rows)
        live["gram"] = (
            joined(2 * rows, 2 * rows + gram_rows),
            joined(2 * rows + gram_rows, 2 * rows + 2 * gram_rows),
        )

        back = dot(live.pop("tall"), with_tangent(resid, tan_resid), 0, 0).astype(BF)
        hv_down = dot(resid, live.pop("tan_hidden"), 1, 1)
        hv_down = live["hv_down"] = hv_down + dot(tan_resid, live["hidden"], 1, 1)
        live["hv_down_b"] = hv_down.astype(BF)

        def lanes(v):
            v = jnp.sum(v, axis=0, keepdims=True)
            return jnp.pad(v, ((0, 0), (0, tokens - v.shape[1])))

        def terms(*values):
            return jnp.concatenate([t for v in values for t in two_terms(v)])

        live["square"] = lanes(hv_down * hv_down)
        got, live = alone(back.reshape(nz, sub, 2 * tokens), "zh", live)
        got = jnp.sum(got.astype(F32), axis=0)
        live["back"] = got[:, :tokens]

        def by_gram(v):
            high, low = live["gram"]
            return dot(v, high, 1, 0) + dot(v, low, 1, 0)

        def deltas(tan_back, tan_gate, tan_upper):
            gate_val, upper, _, _ = live["sums"]
            activated, slope_one, slope_two = silu_parts(gate_val)
            back = live["back"]
            up = tan_back * activated + back * (slope_one * tan_gate)
            gate = (tan_back * upper + back * tan_upper) * slope_one + (
                back * upper
            ) * slope_two * tan_gate
            return jnp.concatenate([gate.astype(BF), up.astype(BF)])

        delta = deltas(got[:, tokens:], *live["sums"][2:])

        tangents = live["tangents"] = by_gram(delta)
        square = lanes(delta.astype(F32) * tangents) + live.pop("square")
        gate_val, upper, _, _ = live["sums"]
        activated, slope_one, _ = silu_parts(gate_val)
        tan_hidden = (
            (slope_one * tangents[:sub]) * upper + activated * tangents[sub:]
        ).astype(BF)
        both, live = gather(jnp.concatenate([tan_hidden, terms(square)]), "zh", nz, live)
        tan_hidden = live["tan_hidden"] = both[:, :sub].reshape(ff, tokens)
        square = jnp.sum(both[:, sub:].astype(F32), axis=(0, 1))[None]

        half = tokens // 2
        out = dot(live["down"], tan_hidden, 1, 0)
        out = (out + dot(live["hv_down_b"], live["hidden"], 1, 0)).astype(BF)
        out = out.reshape(nr, rows, 2, half)
        scal = terms(square[:, :half] + square[:, half:])
        scal = jnp.broadcast_to(scal[None, None], (nr, 1, 2, half))
        got, live = alone(jnp.concatenate([out, scal], axis=1), REST, live)
        got, square = got[:, :rows].astype(F32), got[:, rows:].astype(F32)
        square = jnp.sum(square, axis=(0, 1, 2))[None]
        live["scale"] = 1.0 / jnp.sqrt(total(square, tokens) / count + 1e-6)
        got = jnp.sum(got, axis=0).reshape(rows, tokens)
        tan_resid = (got / tokens).astype(BF)
        tan_resid, live = gather(tan_resid, REST, nr, live)
        tan_resid = tan_resid.reshape(dz, tokens)

        resid = live.pop("resid")
        back = dot(live.pop("down"), tan_resid, 0, 0)
        back = (back + dot(live.pop("hv_down_b"), resid, 0, 0)).astype(BF)
        scale = live.pop("scale")
        hv_down2 = dot(resid, live.pop("tan_hidden"), 1, 1)
        hv_down2 = hv_down2 + dot(tan_resid, live.pop("hidden"), 1, 1)
        hv_down2 = hv_down2 * scale[:, :ff]
        live["inner"] = lanes((live.pop("hv_down") * scale[:, :ff]) * hv_down2)
        live["square"] = lanes(hv_down2 * hv_down2)
        live["hv_down"] = hv_down2.astype(BF)
        live["scale"] = scale
        got, live = alone(back.reshape(nz, sub, tokens), "zh", live)
        got = jnp.sum(got.astype(F32), axis=0)

        scale = live.pop("scale")
        tangents = live.pop("tangents") * scale
        delta = deltas(got * scale, tangents[:sub], tangents[sub:])
        wide = delta.astype(F32)
        inner = lanes(tangents * wide) + live.pop("inner")
        square = lanes(by_gram(delta) * wide) + live.pop("square")
        del live["gram"], live["sums"], live["back"]
        both, live = gather(jnp.concatenate([delta, terms(inner, square)]), "zh", nz, live)
        delta_gate = both[:, :sub].reshape(ff, tokens)
        delta_up = both[:, sub : 2 * sub].reshape(ff, tokens)
        sums = both[:, 2 * sub :].reshape(nz, 2, 2, tokens).astype(F32)
        sums = jnp.sum(sums, axis=(0, 2))
        if tokens > LANES:
            sums = sums[:, :LANES] + sums[:, LANES:]
        sums = jnp.pad(sums, ((0, 0), (0, LANES - sums.shape[1])))
        sums = terms(sums)

        hv = [
            jnp.pad(v.reshape(nx, d_dev, ff), ((0, 0), (0, 0), (0, LANES - ff)))
            for v in (
                dot(live["inputs"], delta_gate, 0, 1).astype(BF),
                dot(live["inputs"], delta_up, 0, 1).astype(BF),
                live["hv_down"],
            )
        ]
        hv.append(jnp.broadcast_to(sums[None], (nx,) + sums.shape))
        got, _ = alone(jnp.concatenate(hv, axis=1), NEAR, ())
        sums = jnp.sum(got[:, 3 * d_dev :].astype(F32), axis=0)
        hv = got[:, : 3 * d_dev, :ff].reshape(nx, 3, d_dev, ff)
        hv = hv.transpose(1, 2, 0, 3).reshape(3, d_dev, ff_dev)
        sums, hv = gather(sums[:2] + sums[2:], ("y", "core"), nt, hv)
        sums = total(jnp.sum(sums, axis=0), ff_dev) / count
        scale = 1.0 / jnp.sqrt(sums[1:] + 1e-6)
        gate, up, down = (v.astype(F32) * scale for v in hv)
        return gate, up, down.T, sums[:1, :1].reshape(())

    return body


def build(devices, sizes):
    wide = Mesh(devices.reshape(sizes), AXES)
    dp, tensor = ("zh", *NEAR), ("y", "core")
    placed = (
        P(dp, tensor),
        P(dp),
        P(None, dp),
        P(dp, tensor),
        P(dp, tensor),
        P(tensor, dp),
        P(dp, tensor),
        P(dp, tensor),
        P(tensor, dp),
    )
    return jax.shard_map(
        make_body(*sizes),
        mesh=wide,
        in_specs=placed,
        out_specs=(P(dp, tensor), P(dp, tensor), P(tensor, dp), P()),
        check_vma=False,
    )


def solution(mesh):
    return build(mesh.devices, SIZES)
```

```python
import functools

import jax
import jax.numpy as jnp
from jax import lax
from jax.experimental import pallas as pl
from jax.experimental.pallas import tpu as pltpu
from jax.sharding import Mesh
from jax.sharding import PartitionSpec as P

AXES = ("zh", "zl", "x", "y", "core")
SIZES = (8, 2, 4, 4, 2)
NEAR = ("zl", "x")
REST = ("zl", "x", "y", "core")
QUAD = ("zl", "x", "y")
LANES = 128
TILE = 16
BF = jnp.bfloat16
F32 = jnp.float32


def dot(a, b, ca, cb):
    return lax.dot_general(a, b, (((ca,), (cb,)), ((), ())), preferred_element_type=F32)


def exchange(v, axes):
    return lax.all_to_all(v, axes, split_axis=0, concat_axis=0, tiled=True)


def alone(v, axes, live):
    v, live = lax.optimization_barrier((v, live))
    return lax.optimization_barrier((exchange(v, axes), live))


def gather(v, axes, n, live):
    return alone(jnp.broadcast_to(v[None], (n,) + v.shape), axes, live)


def two_terms(v):
    high = lax.reduce_precision(v, 8, 7)
    return high.astype(BF), (v - high).astype(BF)


def sibling(v):
    return lax.ppermute(v, "core", [(0, 1), (1, 0)])


def silu_parts(values):
    s = jax.nn.sigmoid(values)
    activated = values * s
    slope_one = s * (1.0 + values * (1.0 - s))
    slope_two = s * (1.0 - s) * (2.0 + values * (1.0 - 2.0 * s))
    return activated, slope_one, slope_two


def total(v, columns):
    ones = jnp.ones((v.shape[1], columns), F32)
    return lax.dot_general(
        v, ones, (((1,), (0,)), ((), ())), precision=lax.Precision.HIGHEST, preferred_element_type=F32
    )


def load_kernel(ff, count, picks, pool, *refs):
    mats, chosen, out = refs[:count], refs[count], refs[count + 1]
    held, near, sem = refs[count + 2 : -2], refs[-2], refs[-1]
    tok_dev = chosen.shape[0]
    copies = []
    for k in range(tok_dev):
        first = pl.multiple_of(picks[k] // TILE * TILE, TILE)
        copies.append(
            pltpu.make_async_copy(pool.at[pl.ds(first, TILE)], near.at[k], sem.at[count + k])
        )
    for m in range(count):
        copies.append(pltpu.make_async_copy(mats[m], held[m], sem.at[m]))
    for copy in copies:
        copy.start()
    for m in range(count):
        copies[tok_dev + m].wait()
        v = held[m][...].astype(F32)
        for e in range(out.shape[0]):
            out[e, m] = v[:, e * ff : (e + 1) * ff].astype(BF)
    picked = []
    for k in range(tok_dev):
        copies[k].wait()
        v = near[k].astype(F32)
        row = lax.broadcasted_iota(jnp.int32, v.shape, 0)
        v = jnp.where(row == picks[k] % TILE, v, 0.0)
        picked.append(jnp.sum(v, axis=0, keepdims=True))
    chosen[...] = jnp.concatenate(picked, axis=0).astype(BF)


def load(picks, pool, mats, parts):
    rows, columns = mats[0].shape
    ff = columns // parts
    tok_dev, width = picks.shape[0], pool.shape[1]
    return pl.pallas_call(
        functools.partial(load_kernel, ff, len(mats)),
        out_shape=[
            jax.ShapeDtypeStruct((tok_dev, width), BF),
            jax.ShapeDtypeStruct((parts, len(mats), rows, ff), BF),
        ],
        in_specs=[pl.BlockSpec(memory_space=pltpu.SMEM)]
        + [pl.BlockSpec(memory_space=pl.ANY)] * (1 + len(mats)),
        out_specs=[pl.BlockSpec(memory_space=pltpu.VMEM)] * 2,
        scratch_shapes=[pltpu.VMEM(m.shape, m.dtype) for m in mats]
        + [
            pltpu.VMEM((tok_dev, TILE, width), BF),
            pltpu.SemaphoreType.DMA((len(mats) + tok_dev,)),
        ],
        compiler_params=pltpu.CompilerParams(vmem_limit_bytes=56 << 20),
        cost_estimate=pl.CostEstimate(flops=0, bytes_accessed=2 << 20, transcendentals=0),
    )(picks, pool, *mats)


def make_body(nz, nl, nx, ny, nc):
    nt = ny * nc
    nx = nl * nx
    nr = nx * nt

    def body(pool, picks, targets, gate_w, up_w, down_w, probe_g, probe_u, probe_d):
        tok_dev = picks.shape[0]
        tokens = targets.shape[0]
        d_dev, ff_dev = gate_w.shape
        ff = ff_dev // nx
        dz = d_dev * nx
        sub = ff // nz
        rows = dz // nr
        nq = nr // nc
        count = 3.0 * (dz * nz) * (ff_dev * nt)

        mats = (gate_w, up_w, probe_g, probe_u, down_w.T, probe_d.T)
        picked, mats = load(picks, pool, mats, nx)
        swap = [(i * nt + j, j * nz + i) for i in range(nz) for j in range(nt)]
        chosen = lax.ppermute(picked, ("zh", "y", "core"), swap)
        mats = exchange(mats, NEAR)

        wanted = targets.reshape(nz, nx, tok_dev, d_dev).transpose(1, 0, 2, 3)
        wanted = wanted.reshape(tokens, d_dev).T
        wanted = lax.dynamic_slice_in_dim(
            wanted, lax.axis_index(("y", "core")) * rows, rows, 0
        )
        mats = mats.transpose(1, 0, 2, 3).reshape(6, dz, ff)
        live = {
            "own": lax.axis_index(REST),
            "wanted": wanted,
            "mats": mats[:4],
            "first": lax.axis_index("core") == 0,
            "down": mats[4],
            "wide": jnp.concatenate([mats[4], mats[5]], axis=1),
            "tall": mats[4:].reshape(2 * dz, ff),
        }
        inputs, live = gather(chosen, REST, nr, live)
        inputs = live["inputs"] = inputs.reshape(tokens, dz)

        first = lax.dot_general(
            live.pop("mats"), inputs, (((1,), (1,)), ((), ())), preferred_element_type=F32
        )
        gram_rows = tokens // nr
        mine = lax.dynamic_slice_in_dim(inputs, live.pop("own") * gram_rows, gram_rows, 0)
        gram = jnp.concatenate(two_terms(dot(mine, inputs, 1, 1)))
        packed = first.astype(BF).reshape(4, nz, sub, tokens).transpose(1, 0, 2, 3)
        packed = packed.reshape(nz, 4 * sub, tokens)
        packed = jnp.concatenate(
            [packed, jnp.broadcast_to(gram[None], (nz,) + gram.shape)], axis=1
        )
        got, live = alone(packed, "zh", live)
        got = jnp.sum(got.astype(F32), axis=0)
        gate_val, upper, tan_gate, tan_upper = (
            got[i * sub : (i + 1) * sub] for i in range(4)
        )
        live["sums"] = (gate_val, upper, tan_gate, tan_upper)
        gram = got[4 * sub : 4 * sub + gram_rows] + got[4 * sub + gram_rows :]
        live["gram"] = jnp.concatenate(two_terms(gram))
        activated, slope_one, _ = silu_parts(gate_val)
        hidden = (activated * upper).astype(BF)
        tan_hidden = (slope_one * tan_gate * upper + activated * tan_upper).astype(BF)
        both, live = gather(jnp.concatenate([hidden, tan_hidden]), "zh", nz, live)
        hidden = live["hidden"] = both[:, :sub].reshape(ff, tokens)
        tan_hidden = live["tan_hidden"] = both[:, sub:].reshape(ff, tokens)

        def with_tangent(v, tan):
            upper = jnp.concatenate([v, tan], axis=1)
            lower = jnp.concatenate([jnp.zeros_like(v), v], axis=1)
            return jnp.concatenate([upper, lower], axis=0)

        out = dot(live.pop("wide"), with_tangent(hidden, tan_hidden), 1, 0).astype(BF)
        got, live = alone(out.reshape(nr, rows, 2 * tokens), REST, live)
        got = jnp.sum(got.astype(F32), axis=0)
        out, tan_out = got[:, :tokens], got[:, tokens:]
        resid = ((out - live.pop("wanted").astype(F32)) / tokens).astype(BF)
        tan_resid = (tan_out / tokens).astype(BF)
        packed = jnp.concatenate([resid, tan_resid, live.pop("gram")])
        mine, live = gather(packed, QUAD, nq, live)
        other, first = sibling(mine), live.pop("first")
        both = jnp.stack([jnp.where(first, mine, other), jnp.where(first, other, mine)], axis=1)

        def joined(start, stop):
            return both[:, :, start:stop].reshape(nr * (stop - start), tokens)

        resid = live["resid"] = joined(0, rows)
        tan_resid = joined(rows, 2 * rows)
        live["gram"] = (
            joined(2 * rows, 2 * rows + gram_rows),
            joined(2 * rows + gram_rows, 2 * rows + 2 * gram_rows),
        )

        back = dot(live.pop("tall"), with_tangent(resid, tan_resid), 0, 0).astype(BF)
        hv_down = dot(resid, live.pop("tan_hidden"), 1, 1)
        hv_down = live["hv_down"] = hv_down + dot(tan_resid, live["hidden"], 1, 1)
        live["hv_down_b"] = hv_down.astype(BF)

        def lanes(v):
            v = jnp.sum(v, axis=0, keepdims=True)
            return jnp.pad(v, ((0, 0), (0, tokens - v.shape[1])))

        def wide_lanes(v):
            return jnp.sum(jnp.sum(v, axis=1).reshape(-1, tokens), axis=0, keepdims=True)

        def terms(*values):
            return jnp.concatenate([t for v in values for t in two_terms(v)])

        live["square"] = wide_lanes(hv_down * hv_down)
        got, live = alone(back.reshape(nz, sub, 2 * tokens), "zh", live)
        got = jnp.sum(got.astype(F32), axis=0)
        live["back"] = got[:, :tokens]

        def by_gram(v):
            high, low = live["gram"]
            return dot(v, high, 1, 0) + dot(v, low, 1, 0)

        def deltas(tan_back, tan_gate, tan_upper):
            gate_val, upper, _, _ = live["sums"]
            activated, slope_one, slope_two = silu_parts(gate_val)
            back = live["back"]
            up = tan_back * activated + back * (slope_one * tan_gate)
            gate = (tan_back * upper + back * tan_upper) * slope_one + (
                back * upper
            ) * slope_two * tan_gate
            return jnp.concatenate([gate.astype(BF), up.astype(BF)])

        delta = deltas(got[:, tokens:], *live["sums"][2:])

        tangents = live["tangents"] = by_gram(delta)
        square = lanes(delta.astype(F32) * tangents) + live.pop("square")
        gate_val, upper, _, _ = live["sums"]
        activated, slope_one, _ = silu_parts(gate_val)
        tan_hidden = (
            (slope_one * tangents[:sub]) * upper + activated * tangents[sub:]
        ).astype(BF)
        both, live = gather(jnp.concatenate([tan_hidden, terms(square)]), "zh", nz, live)
        tan_hidden = live["tan_hidden"] = both[:, :sub].reshape(ff, tokens)
        square = jnp.sum(both[:, sub:].astype(F32), axis=(0, 1))[None]

        half = tokens // 2
        live["square"] = terms(square[:, :half] + square[:, half:])
        out = dot(live["down"], tan_hidden, 1, 0)
        out = (out + dot(live["hv_down_b"], live["hidden"], 1, 0)).astype(BF)
        got, live = alone(out.reshape(nr, rows, tokens), REST, live)
        tan_resid = (jnp.sum(got.astype(F32), axis=0) / tokens).astype(BF)
        packed = tan_resid.reshape(rows, 2, half)
        packed = jnp.concatenate([packed, live.pop("square")[None]])
        both, live = gather(packed, REST, nr, live)
        tan_resid = both[:, :rows].reshape(dz, tokens)
        square = jnp.sum(both[:, rows:].astype(F32), axis=(0, 1, 2))[None]
        live["scale"] = 1.0 / jnp.sqrt(total(square, tokens) / count + 1e-6)

        resid = live.pop("resid")
        back = dot(live.pop("down"), tan_resid, 0, 0)
        back = (back + dot(live.pop("hv_down_b"), resid, 0, 0)).astype(BF)
        scale = live.pop("scale")
        hv_down2 = dot(resid, live.pop("tan_hidden"), 1, 1)
        hv_down2 = hv_down2 + dot(tan_resid, live.pop("hidden"), 1, 1)
        hv_down2 = hv_down2 * scale[:, :ff]
        live["inner"] = wide_lanes((live.pop("hv_down") * scale[:, :ff]) * hv_down2)
        live["square"] = wide_lanes(hv_down2 * hv_down2)
        live["hv_down"] = hv_down2.astype(BF)
        live["scale"] = scale
        got, live = alone(back.reshape(nz, sub, tokens), "zh", live)
        got = jnp.sum(got.astype(F32), axis=0)

        scale = live.pop("scale")
        tangents = live.pop("tangents") * scale
        delta = deltas(got * scale, tangents[:sub], tangents[sub:])
        wide = delta.astype(F32)
        inner = lanes(tangents * wide) + live.pop("inner")
        square = lanes(by_gram(delta) * wide) + live.pop("square")
        del live["gram"], live["sums"], live["back"]
        both, live = gather(jnp.concatenate([delta, terms(inner, square)]), "zh", nz, live)
        delta_gate = both[:, :sub].reshape(ff, tokens)
        delta_up = both[:, sub : 2 * sub].reshape(ff, tokens)
        sums = both[:, 2 * sub :].reshape(nz, 2, 2, tokens).astype(F32)
        sums = jnp.sum(sums, axis=(0, 2))
        if tokens > LANES:
            sums = sums[:, :LANES] + sums[:, LANES:]
        sums = jnp.pad(sums, ((0, 0), (0, LANES - sums.shape[1])))
        sums = terms(sums)

        hv = [
            jnp.pad(v.reshape(nx, d_dev, ff), ((0, 0), (0, 0), (0, LANES - ff)))
            for v in (
                dot(live["inputs"], delta_gate, 0, 1).astype(BF),
                dot(live["inputs"], delta_up, 0, 1).astype(BF),
                live["hv_down"],
            )
        ]
        hv.append(jnp.broadcast_to(sums[None], (nx,) + sums.shape))
        got, _ = alone(jnp.concatenate(hv, axis=1), NEAR, ())
        sums = jnp.sum(got[:, 3 * d_dev :].astype(F32), axis=0)
        hv = got[:, : 3 * d_dev, :ff].reshape(nx, 3, d_dev, ff)
        hv = hv.transpose(1, 2, 0, 3).reshape(3, d_dev, ff_dev)
        sums, hv = gather(sums[:2] + sums[2:], ("y", "core"), nt, hv)
        sums = total(jnp.sum(sums, axis=0), ff_dev) / count
        scale = 1.0 / jnp.sqrt(sums[1:] + 1e-6)
        gate, up, down = (v.astype(F32) * scale for v in hv)
        return gate, up, down.T, sums[:1, :1].reshape(())

    return body


def build(devices, sizes):
    wide = Mesh(devices.reshape(sizes), AXES)
    dp, tensor = ("zh", *NEAR), ("y", "core")
    placed = (
        P(dp, tensor),
        P(dp),
        P(None, dp),
        P(dp, tensor),
        P(dp, tensor),
        P(tensor, dp),
        P(dp, tensor),
        P(dp, tensor),
        P(tensor, dp),
    )
    return jax.shard_map(
        make_body(*sizes),
        mesh=wide,
        in_specs=placed,
        out_specs=(P(dp, tensor), P(dp, tensor), P(tensor, dp), P()),
        check_vma=False,
    )


def solution(mesh):
    return build(mesh.devices, SIZES)
```

```python
import functools

import jax
import jax.numpy as jnp
from jax import lax
from jax.experimental import pallas as pl
from jax.experimental.pallas import tpu as pltpu
from jax.sharding import Mesh
from jax.sharding import PartitionSpec as P

AXES = ("zh", "zl", "x", "y", "core")
SIZES = (8, 2, 4, 4, 2)
NEAR = ("zl", "x")
REST = ("zl", "x", "y", "core")
QUAD = ("zl", "x", "y")
LANES = 128
TILE = 16
BF = jnp.bfloat16
F32 = jnp.float32


def dot(a, b, ca, cb):
    return lax.dot_general(a, b, (((ca,), (cb,)), ((), ())), preferred_element_type=F32)


def exchange(v, axes):
    return lax.all_to_all(v, axes, split_axis=0, concat_axis=0, tiled=True)


def alone(v, axes, live):
    v, live = lax.optimization_barrier((v, live))
    return lax.optimization_barrier((exchange(v, axes), live))


def gather(v, axes, n, live):
    return alone(jnp.broadcast_to(v[None], (n,) + v.shape), axes, live)


def two_terms(v):
    high = lax.reduce_precision(v, 8, 7)
    return high.astype(BF), (v - high).astype(BF)


def sibling(v):
    return lax.ppermute(v, "core", [(0, 1), (1, 0)])


def silu_parts(values):
    s = jax.nn.sigmoid(values)
    activated = values * s
    slope_one = s * (1.0 + values * (1.0 - s))
    slope_two = s * (1.0 - s) * (2.0 + values * (1.0 - 2.0 * s))
    return activated, slope_one, slope_two


def total(v, columns):
    ones = jnp.ones((v.shape[1], columns), F32)
    return lax.dot_general(
        v, ones, (((1,), (0,)), ((), ())), precision=lax.Precision.HIGHEST, preferred_element_type=F32
    )


def load_kernel(ff, count, picks, pool, *refs):
    mats, chosen, out = refs[:count], refs[count], refs[count + 1]
    held, near, sem = refs[count + 2 : -2], refs[-2], refs[-1]
    tok_dev = chosen.shape[0]
    copies = []
    for k in range(tok_dev):
        first = pl.multiple_of(picks[k] // TILE * TILE, TILE)
        copies.append(
            pltpu.make_async_copy(pool.at[pl.ds(first, TILE)], near.at[k], sem.at[count + k])
        )
    for m in range(count):
        copies.append(pltpu.make_async_copy(mats[m], held[m], sem.at[m]))
    for copy in copies:
        copy.start()
    for m in range(count):
        copies[tok_dev + m].wait()
        v = held[m][...].astype(F32)
        for e in range(out.shape[0]):
            out[e, m] = v[:, e * ff : (e + 1) * ff].astype(BF)
    picked = []
    for k in range(tok_dev):
        copies[k].wait()
        v = near[k].astype(F32)
        row = lax.broadcasted_iota(jnp.int32, v.shape, 0)
        v = jnp.where(row == picks[k] % TILE, v, 0.0)
        picked.append(jnp.sum(v, axis=0, keepdims=True))
    chosen[...] = jnp.concatenate(picked, axis=0).astype(BF)


def load(picks, pool, mats, parts):
    rows, columns = mats[0].shape
    ff = columns // parts
    tok_dev, width = picks.shape[0], pool.shape[1]
    return pl.pallas_call(
        functools.partial(load_kernel, ff, len(mats)),
        out_shape=[
            jax.ShapeDtypeStruct((tok_dev, width), BF),
            jax.ShapeDtypeStruct((parts, len(mats), rows, ff), BF),
        ],
        in_specs=[pl.BlockSpec(memory_space=pltpu.SMEM)]
        + [pl.BlockSpec(memory_space=pl.ANY)] * (1 + len(mats)),
        out_specs=[pl.BlockSpec(memory_space=pltpu.VMEM)] * 2,
        scratch_shapes=[pltpu.VMEM(m.shape, m.dtype) for m in mats]
        + [
            pltpu.VMEM((tok_dev, TILE, width), BF),
            pltpu.SemaphoreType.DMA((len(mats) + tok_dev,)),
        ],
        compiler_params=pltpu.CompilerParams(vmem_limit_bytes=56 << 20),
        cost_estimate=pl.CostEstimate(flops=0, bytes_accessed=2 << 20, transcendentals=0),
    )(picks, pool, *mats)


def make_body(nz, nl, nx, ny, nc):
    nt = ny * nc
    nx = nl * nx
    nr = nx * nt

    def body(pool, picks, targets, gate_w, up_w, down_w, probe_g, probe_u, probe_d):
        tok_dev = picks.shape[0]
        tokens = targets.shape[0]
        d_dev, ff_dev = gate_w.shape
        ff = ff_dev // nx
        dz = d_dev * nx
        sub = ff // nz
        rows = dz // nr
        nq = nr // nc
        count = 3.0 * (dz * nz) * (ff_dev * nt)

        mats = (gate_w, up_w, probe_g, probe_u, down_w.T, probe_d.T)
        picked, mats = load(picks, pool, mats, nx)
        swap = [(i * nt + j, j * nz + i) for i in range(nz) for j in range(nt)]
        chosen = lax.ppermute(picked, ("zh", "y", "core"), swap)
        mats = exchange(mats, NEAR)

        wanted = targets.reshape(nz, nx, tok_dev, d_dev).transpose(1, 0, 2, 3)
        wanted = wanted.reshape(tokens, d_dev).T
        wanted = lax.dynamic_slice_in_dim(
            wanted, lax.axis_index(("y", "core")) * rows, rows, 0
        )
        mats = mats.transpose(1, 0, 2, 3).reshape(6, dz, ff)
        live = {
            "own": lax.axis_index(REST),
            "wanted": wanted,
            "mats": mats[:4],
            "first": lax.axis_index("core") == 0,
            "down": mats[4],
            "wide": jnp.concatenate([mats[4], mats[5]], axis=1),
            "tall": mats[4:].reshape(2 * dz, ff),
        }
        inputs, live = gather(chosen, REST, nr, live)
        inputs = live["inputs"] = inputs.reshape(tokens, dz)

        first = lax.dot_general(
            live.pop("mats"), inputs, (((1,), (1,)), ((), ())), preferred_element_type=F32
        )
        gram_rows = tokens // nr
        mine = lax.dynamic_slice_in_dim(inputs, live.pop("own") * gram_rows, gram_rows, 0)
        gram = jnp.concatenate(two_terms(dot(mine, inputs, 1, 1)))
        packed = first.astype(BF).reshape(4, nz, sub, tokens).transpose(1, 0, 2, 3)
        packed = packed.reshape(nz, 4 * sub, tokens)
        packed = jnp.concatenate(
            [packed, jnp.broadcast_to(gram[None], (nz,) + gram.shape)], axis=1
        )
        got, live = alone(packed, "zh", live)
        got = jnp.sum(got.astype(F32), axis=0)
        gate_val, upper, tan_gate, tan_upper = (
            got[i * sub : (i + 1) * sub] for i in range(4)
        )
        live["sums"] = (gate_val, upper, tan_gate, tan_upper)
        gram = got[4 * sub : 4 * sub + gram_rows] + got[4 * sub + gram_rows :]
        live["gram"] = jnp.concatenate(two_terms(gram))
        activated, slope_one, _ = silu_parts(gate_val)
        hidden = (activated * upper).astype(BF)
        tan_hidden = (slope_one * tan_gate * upper + activated * tan_upper).astype(BF)
        both, live = gather(jnp.concatenate([hidden, tan_hidden]), "zh", nz, live)
        hidden = live["hidden"] = both[:, :sub].reshape(ff, tokens)
        tan_hidden = live["tan_hidden"] = both[:, sub:].reshape(ff, tokens)

        def with_tangent(v, tan):
            upper = jnp.concatenate([v, tan], axis=1)
            lower = jnp.concatenate([jnp.zeros_like(v), v], axis=1)
            return jnp.concatenate([upper, lower], axis=0)

        out = dot(live.pop("wide"), with_tangent(hidden, tan_hidden), 1, 0).astype(BF)
        got, live = alone(out.reshape(nr, rows, 2 * tokens), REST, live)
        got = jnp.sum(got.astype(F32), axis=0)
        out, tan_out = got[:, :tokens], got[:, tokens:]
        resid = ((out - live.pop("wanted").astype(F32)) / tokens).astype(BF)
        tan_resid = (tan_out / tokens).astype(BF)
        packed = jnp.concatenate([resid, tan_resid, live.pop("gram")])
        mine, live = gather(packed, QUAD, nq, live)
        other, first = sibling(mine), live.pop("first")
        both = jnp.stack([jnp.where(first, mine, other), jnp.where(first, other, mine)], axis=1)

        def joined(start, stop):
            return both[:, :, start:stop].reshape(nr * (stop - start), tokens)

        resid = live["resid"] = joined(0, rows)
        tan_resid = joined(rows, 2 * rows)
        live["gram"] = (
            joined(2 * rows, 2 * rows + gram_rows),
            joined(2 * rows + gram_rows, 2 * rows + 2 * gram_rows),
        )

        back = dot(live.pop("tall"), with_tangent(resid, tan_resid), 0, 0).astype(BF)
        hv_down = dot(resid, live.pop("tan_hidden"), 1, 1)
        hv_down = live["hv_down"] = hv_down + dot(tan_resid, live["hidden"], 1, 1)
        live["hv_down_b"] = hv_down.astype(BF)

        def lanes(v):
            v = jnp.sum(v, axis=0, keepdims=True)
            return jnp.pad(v, ((0, 0), (0, tokens - v.shape[1])))

        def wide_lanes(v):
            return jnp.sum(jnp.sum(v, axis=1).reshape(-1, tokens), axis=0, keepdims=True)

        def terms(*values):
            return jnp.concatenate([t for v in values for t in two_terms(v)])

        live["square"] = wide_lanes(hv_down * hv_down)
        got, live = alone(back.reshape(nz, sub, 2 * tokens), "zh", live)
        got = jnp.sum(got.astype(F32), axis=0)
        live["back"] = got[:, :tokens]

        def by_gram(v):
            high, low = live["gram"]
            return dot(v, high, 1, 0) + dot(v, low, 1, 0)

        def deltas(tan_back, tan_gate, tan_upper):
            gate_val, upper, _, _ = live["sums"]
            activated, slope_one, slope_two = silu_parts(gate_val)
            back = live["back"]
            up = tan_back * activated + back * (slope_one * tan_gate)
            gate = (tan_back * upper + back * tan_upper) * slope_one + (
                back * upper
            ) * slope_two * tan_gate
            return jnp.concatenate([gate.astype(BF), up.astype(BF)])

        delta = deltas(got[:, tokens:], *live["sums"][2:])

        tangents = live["tangents"] = by_gram(delta)
        square = lanes(delta.astype(F32) * tangents) + live.pop("square")
        gate_val, upper, _, _ = live["sums"]
        activated, slope_one, _ = silu_parts(gate_val)
        tan_hidden = (
            (slope_one * tangents[:sub]) * upper + activated * tangents[sub:]
        ).astype(BF)
        both, live = gather(jnp.concatenate([tan_hidden, terms(square)]), "zh", nz, live)
        tan_hidden = live["tan_hidden"] = both[:, :sub].reshape(ff, tokens)
        square = jnp.sum(both[:, sub:].astype(F32), axis=(0, 1))[None]

        half = tokens // 2
        live["square"] = terms(square[:, :half] + square[:, half:])
        out = dot(live["down"], tan_hidden, 1, 0)
        out = (out + dot(live["hv_down_b"], live["hidden"], 1, 0)).astype(BF)
        got, live = alone(out.reshape(nr, rows, tokens), REST, live)
        tan_resid = (jnp.sum(got.astype(F32), axis=0) / tokens).astype(BF)
        packed = tan_resid.reshape(rows, 2, half)
        packed = jnp.concatenate([packed, live.pop("square")[None]])
        both, live = gather(packed, REST, nr, live)
        tan_resid = both[:, :rows].reshape(dz, tokens)
        square = jnp.sum(both[:, rows:].astype(F32), axis=(0, 1, 2))[None]
        live["scale"] = 1.0 / jnp.sqrt(total(square, tokens) / count + 1e-6)

        resid = live.pop("resid")
        back = dot(live.pop("down"), tan_resid, 0, 0)
        back = (back + dot(live.pop("hv_down_b"), resid, 0, 0)).astype(BF)
        scale = live.pop("scale")
        hv_down2 = dot(resid, live.pop("tan_hidden"), 1, 1)
        hv_down2 = hv_down2 + dot(tan_resid, live.pop("hidden"), 1, 1)
        hv_down2 = hv_down2 * scale[:, :ff]
        live["inner"] = wide_lanes((live.pop("hv_down") * scale[:, :ff]) * hv_down2)
        live["square"] = wide_lanes(hv_down2 * hv_down2)
        live["hv_down"] = hv_down2.astype(BF)
        live["scale"] = scale
        got, live = alone(back.reshape(nz, sub, tokens), "zh", live)
        got = jnp.sum(got.astype(F32), axis=0)

        scale = live.pop("scale")
        tangents = live.pop("tangents") * scale
        delta = deltas(got * scale, tangents[:sub], tangents[sub:])
        wide = delta.astype(F32)
        inner = lanes(tangents * wide) + live.pop("inner")
        square = lanes(by_gram(delta) * wide) + live.pop("square")
        del live["gram"], live["sums"], live["back"]
        both, live = gather(jnp.concatenate([delta, terms(inner, square)]), "zh", nz, live)
        delta = both[:, : 2 * sub].reshape(nz, 2, sub, tokens).transpose(1, 0, 2, 3)
        hv = dot(delta.reshape(2 * ff, tokens), live["inputs"], 1, 0).astype(BF)
        hv = hv.reshape(2, ff, dz).transpose(0, 2, 1)
        sums = both[:, 2 * sub :].reshape(nz, 2, 2, tokens).astype(F32)
        sums = jnp.sum(sums, axis=(0, 2))
        if tokens > LANES:
            sums = sums[:, :LANES] + sums[:, LANES:]
        sums = jnp.pad(sums, ((0, 0), (0, LANES - sums.shape[1])))
        sums = terms(sums)

        hv = [
            jnp.pad(v.reshape(nx, d_dev, ff), ((0, 0), (0, 0), (0, LANES - ff)))
            for v in (
                hv[0],
                hv[1],
                live["hv_down"],
            )
        ]
        hv.append(jnp.broadcast_to(sums[None], (nx,) + sums.shape))
        got, _ = alone(jnp.concatenate(hv, axis=1), NEAR, ())
        sums = jnp.sum(got[:, 3 * d_dev :].astype(F32), axis=0)
        hv = got[:, : 3 * d_dev, :ff].reshape(nx, 3, d_dev, ff)
        hv = hv.transpose(1, 2, 0, 3).reshape(3, d_dev, ff_dev)
        sums, hv = gather(sums[:2] + sums[2:], ("y", "core"), nt, hv)
        sums = total(jnp.sum(sums, axis=0), ff_dev) / count
        scale = 1.0 / jnp.sqrt(sums[1:] + 1e-6)
        gate, up, down = (v.astype(F32) * scale for v in hv)
        return gate, up, down.T, sums[:1, :1].reshape(())

    return body


def build(devices, sizes):
    wide = Mesh(devices.reshape(sizes), AXES)
    dp, tensor = ("zh", *NEAR), ("y", "core")
    placed = (
        P(dp, tensor),
        P(dp),
        P(None, dp),
        P(dp, tensor),
        P(dp, tensor),
        P(tensor, dp),
        P(dp, tensor),
        P(dp, tensor),
        P(tensor, dp),
    )
    return jax.shard_map(
        make_body(*sizes),
        mesh=wide,
        in_specs=placed,
        out_specs=(P(dp, tensor), P(dp, tensor), P(tensor, dp), P()),
        check_vma=False,
    )


def solution(mesh):
    return build(mesh.devices, SIZES)
```
